256 devices in a mesh: dp: 16 (over x_hi, z), tensor: 16 (over y, x_lo, core).
Axes of the slice: x: 4 (x_hi: 2, x_lo: 2; x = x_hi * 2 + x_lo), y: 4, z: 8, core: 2. Of those that a mesh axis runs over, the one named last changes fastest.
Arguments:
- hidden_in: bfloat16 [4096, 12288], P('dp', 'tensor'), as said below
- residual_grad: bfloat16 [4096, 12288], P('dp', 'tensor'), may hold values from -6 to 6
- key_value_gradient: bfloat16 [4096, 2048], P('dp', 'tensor'), as said below
- shortcut: bfloat16 [12288, 12288], P('dp', 'tensor'), may hold values from -0.02734375 to 0.02734375
- key_value_weight: bfloat16 [12288, 2048], P('dp', 'tensor'), as said below
- adapter_down_matrix: float32 [12288, 64], replicated, may hold values from -0.0546875 to 0.0546875
- adapter_up: float32 [64, 2048], replicated, may hold values from -0.75 to 0.75
Outputs:
- input_grad: bfloat16 [4096, 12288], P(('dp', 'tensor'))
- adapter_down_grad: float32 [12288, 64], replicated
- adapter_up_grad: float32 [64, 2048], replicated
The draws below stay inside these ranges and needn't reach their ends.
Inputs may be any that keep to these rules, and one draw needn't show every extreme that they name: `hidden_in`: entries are finite; token rows and feature columns have unlike scales. `key_value_gradient`: entries are finite. `key_value_weight`: entries are finite.
All inputs are finite; a program needn't handle non-finite values.
Results may differ from the reference program's by a relative error of at most 0.0095.
Values may be sent and summed in bfloat16 or wider, within the bound.
A program may use at most 128 MiB of HBM per device.

```python
import jax
import jax.numpy as jnp
from jax import lax

D = 12288
KVW = 2048
RANK = 64
TOKENS = 4096


def shared_core(key):
    return jax.random.normal(jax.random.fold_in(key, 101), (TOKENS, D), jnp.float32)


def paired_features(key):
    stride = D // KVW
    offsets = jax.random.randint(jax.random.fold_in(key, 202), (KVW,), 0, stride)
    return jnp.arange(KVW, dtype=jnp.int32) * stride + offsets.astype(jnp.int32)


def draw_hidden_in(key, part):
    core = shared_core(key)
    key = jax.random.fold_in(key, 11)
    keys = jax.random.split(key, 2)
    row_scale = 0.1 * jnp.exp(jax.random.uniform(keys[0], (TOKENS, 1), jnp.float32) * jnp.log(10.0))
    trend = jnp.exp(0.5 * jnp.log(3.0) * jnp.arange(D, dtype=jnp.float32) / (D - 1))
    col_scale = jnp.exp(jax.random.uniform(keys[1], (1, D), jnp.float32) * jnp.log(10.0)) * trend[None, :]
    return (core * row_scale * col_scale).astype(jnp.bfloat16)


def draw_key_value_gradient(key, part):
    core = shared_core(key)
    paired = paired_features(key)
    key = jax.random.fold_in(key, 12)
    fresh_values = jax.random.normal(key, (TOKENS, KVW), jnp.float32)
    picked = jnp.take(core, paired, axis=1)
    return (0.35 * fresh_values + 0.95 * picked).astype(jnp.bfloat16)


def draw_key_value_weight(key, part):
    paired = paired_features(key)
    key = jax.random.fold_in(key, 13)
    keys = jax.random.split(key, 2)
    dense_part = jax.random.normal(keys[0], (D, KVW), jnp.float32) * D ** (-0.5)
    strength = jax.random.uniform(keys[1], (1, KVW), jnp.float32, 2.5, 4.5)
    pairing_mask = (jnp.arange(D, dtype=jnp.int32)[:, None] == paired[None, :]).astype(jnp.float32)
    return (dense_part + pairing_mask * strength).astype(jnp.bfloat16)


def level_of(key, shape, cuts, low, largest):
    gain = 1.0
    for dim, parts in cuts:
        draws = jax.random.uniform(jax.random.fold_in(jax.random.fold_in(key, 6), dim), (parts,), jnp.float32, low / len(cuts), largest / len(cuts))
        gain = gain * jnp.repeat(jnp.exp(draws), shape[dim] // parts).reshape((-1,) + (1,) * (len(shape) - 1 - dim))
    return gain


def normal_values(key, dims, deviation, most, cuts=(), kind=jnp.bfloat16):
    array = deviation * jax.random.normal(key, dims, jnp.float32)
    if cuts:
        array = array * level_of(key, dims, cuts, -0.22, 0.18)
    return jnp.clip(array, -most, most).astype(kind)


def setup_inputs(seed: int = 0) -> dict:
    splits = jax.random.split(jax.random.key(seed), 8)
    return {
        "hidden_in": draw_hidden_in(jax.random.fold_in(splits[7], 71), 0),
        "residual_grad": normal_values(splits[1], (TOKENS, D), 1.0, 6.0, ((0, 16), (1, 16))),
        "key_value_gradient": draw_key_value_gradient(jax.random.fold_in(splits[7], 71), 0),
        "shortcut": normal_values(splits[3], (D, D), (4 * D) ** -0.5, 0.02734375, ((0, 16), (1, 16))),
        "key_value_weight": draw_key_value_weight(jax.random.fold_in(splits[7], 71), 0),
        "adapter_down_matrix": normal_values(splits[5], (D, RANK), D ** -0.5, 0.0546875, (), jnp.float32),
        "adapter_up": normal_values(splits[6], (RANK, KVW), RANK ** -0.5, 0.75, (), jnp.float32),
    }


epsilon = 1e-05
adapter_scale = 0.25

def contract_final_axis(left, right):
    return lax.dot_general(left, right, (((1,), (1,)), ((), ())), preferred_element_type=jnp.float32)

def reference(hidden_in, residual_grad, key_value_gradient, shortcut, key_value_weight, adapter_down_matrix, adapter_up):
    highest_precision = lax.Precision.HIGHEST
    inputs32 = hidden_in.astype(jnp.float32)
    scale_row = lax.rsqrt(lax.optimization_barrier(jnp.mean(inputs32 * inputs32, axis=1)) + epsilon)
    normalized_input = inputs32 * scale_row[:, None]
    key_value_float32 = key_value_gradient.astype(jnp.float32)
    low_rank_product = jnp.dot(normalized_input, adapter_down_matrix, precision=highest_precision)
    backward_value = jnp.dot(key_value_float32, adapter_up.T, precision=highest_precision)
    up_gradient = adapter_scale * jnp.dot(low_rank_product.T, key_value_float32, precision=highest_precision)
    down_gradient = adapter_scale * jnp.dot(normalized_input.T, backward_value, precision=highest_precision)
    short_part = contract_final_axis(residual_grad, shortcut)
    gradient_norm = contract_final_axis(key_value_gradient, key_value_weight) + adapter_scale * jnp.dot(backward_value, adapter_down_matrix.T, precision=highest_precision)
    inner = lax.optimization_barrier(jnp.mean(gradient_norm * normalized_input, axis=1, keepdims=True))
    result = short_part + scale_row[:, None] * (gradient_norm - normalized_input * inner)
    return (result.astype(jnp.bfloat16), down_gradient, up_gradient)
```

```python
import jax
import jax.numpy as jnp
from jax import lax
from jax.experimental import pallas as pl
from jax.experimental.pallas import tpu as pltpu
from jax.sharding import PartitionSpec as P

MESH = pl.DeviceIdType.MESH
UNITS = 16
LAG = 2
PIECES = 4


def place(xh, z, y, xl, c):
    return {"dp": xh * 8 + z, "tensor": (y * 2 + xl) * 2 + c}


def contract(a, b):
    return lax.dot_general(a, b, (((1,), (1,)), ((), ())), preferred_element_type=jnp.float32)


def short_kernel(
    grad_ref, short_ref, out_ref,
    blocks, weights, relay, core_out, core_in, own, y_out, y_in, pair, x_out, x_in, fin_out, fin_in,
    load_sem, a_send, a_recv, s_send, s_recv, r_send, r_recv,
    core_send, core_recv, y_send, y_recv, x_send, x_recv, f_send, f_recv,
):
    p, q = lax.axis_index("dp"), lax.axis_index("tensor")
    xh, z = p // 8, p % 8
    y, xl, c = q // 4, (q // 2) % 2, q % 2
    x = xh * 2 + xl
    xp, xm = (x + 1) % 4, (x + 3) % 4

    def at(xh=xh, z=z, y=y, xl=xl, c=c):
        return place(xh, z, y, xl, c)

    right, left = at(xh=xp // 2, xl=xp % 2), at(xh=xm // 2, xl=xm % 2)
    up, down = at(z=(z + 1) % 8), at(z=(z + 7) % 8)
    core_peer = at(c=1 - c)
    xl_peer = at(xl=1 - xl)

    loads = [pltpu.make_async_copy(grad_ref.at[:, h], blocks.at[0, h], load_sem.at[h]) for h in range(2)]
    loads.append(pltpu.make_async_copy(short_ref, weights.at[0], load_sem.at[2]))
    for l in loads:
        l.start()

    barrier = pltpu.get_barrier_semaphore()
    peers = [core_peer, right, left] + [at(y=(y + d) % 4) for d in (1, 2, 3)] + [at(z=(z + d) % 8) for d in range(1, 8)]
    for peer in peers:
        pl.semaphore_signal(barrier, inc=1, device_id=peer, device_id_type=MESH)
    for l in loads:
        l.wait()
    pl.semaphore_wait(barrier, len(peers))

    def remote(src, dst, send, recv, to):
        return pltpu.make_async_remote_copy(
            src_ref=src, dst_ref=dst, send_sem=send, recv_sem=recv, device_id=to, device_id_type=MESH
        )

    rows = 384 // PIECES

    def swap_copy(way, n):
        lo = way * 384 + n * rows
        i = way * PIECES + n
        return remote(
            weights.at[0, pl.ds(lo, rows)], relay.at[i], s_send.at[i], s_recv.at[i], (right, left)[way]
        )

    def relay_copy(way, n):
        lo = way * 384 + n * rows
        i = way * PIECES + n
        return remote(
            relay.at[i], weights.at[1, pl.ds(lo, rows)], r_send.at[i], r_recv.at[i], (right, left)[way]
        )

    def block_copy(k):
        if k == 7:
            return remote(blocks.at[5, 0], blocks.at[7, 0], a_send.at[7], a_recv.at[7], up)
        if k == 8:
            return remote(blocks.at[6, 1], blocks.at[7, 1], a_send.at[8], a_recv.at[8], down)
        source = max(k - 2, 0)
        return remote(blocks.at[source], blocks.at[k], a_send.at[k], a_recv.at[k], up if k % 2 else down)

    block_copy(1).start()
    block_copy(2).start()
    for n in range(PIECES):
        for way in range(2):
            swap_copy(way, n).start()

    def core_copy(i):
        return remote(core_out.at[i], core_in.at[i], core_send.at[i], core_recv.at[i], core_peer)

    def y_copy(i, d):
        to = (y + d) % 4
        return remote(y_out.at[i, to], y_in.at[i, d - 1], y_send.at[i, d - 1], y_recv.at[i, d - 1], at(y=to))

    def x_copy(i):
        return remote(x_out.at[i], x_in.at[i], x_send.at[i], x_recv.at[i], xl_peer)

    def fin_slot(i):
        g = i // 8
        return (xh + g - 2 * xh * g) * 8 + z

    def fin_copy(i, to_z):
        s = fin_slot(i)
        return remote(fin_out.at[i], fin_in.at[s], f_send.at[i], f_recv.at[s], at(z=to_z))

    def block_z(k):
        half = (k + 1) // 2
        return lax.rem(z + 8 + half - 2 * half * (k % 2), 8)

    def slot(i, carry):
        for k in range(1, 8):
            @pl.when(i == k)
            def _():
                block_copy(k).wait_recv()
                if k == 7:
                    block_copy(8).wait_recv()
                if k <= 4:
                    block_copy(k + 2).start()
                elif k <= 6:
                    block_copy(k + 2).start()
                if 1 <= k <= PIECES:
                    for way in range(2):
                        swap_copy(way, k - 1).wait_recv()
                        relay_copy(way, k - 1).start()

        @pl.when(i == 8)
        def _():
            for n in range(PIECES):
                for way in range(2):
                    relay_copy(way, n).wait_recv()

        @pl.when(i < UNITS)
        def _():
            k, g = i % 8, i // 8
            theirs = contract(blocks[k, 1 - c].reshape(128, 768), weights[g])
            core_out[i] = theirs.astype(jnp.bfloat16).reshape(4, 32, 768)
            core_copy(i).start()
            own[i] = contract(blocks[k, c].reshape(128, 768), weights[g]).reshape(4, 32, 768)

        j = i - LAG

        @pl.when(jnp.logical_and(j >= 0, j < UNITS))
        def _():
            core_copy(j).wait_recv()
            total = own[j] + core_in[j].astype(jnp.float32)
            own[j] = total
            y_out[j] = total.astype(jnp.bfloat16)
            for d in (2, 1, 3):
                y_copy(j, d).start()

        m = i - 2 * LAG

        @pl.when(jnp.logical_and(m >= 0, m < UNITS))
        def _():
            for d in (1, 2, 3):
                y_copy(m, d).wait_recv()
            got = y_in[m].astype(jnp.float32)
            total = ((own[m, y] + got[0]) + (got[1] + got[2])).reshape(2, 16, 768)
            pair[m] = total
            x_out[m] = pair[m, 1 - xl].astype(jnp.bfloat16)
            x_copy(m).start()

        n = i - 3 * LAG

        @pl.when(jnp.logical_and(n >= 0, n < UNITS))
        def _():
            x_copy(n).wait_recv()
            done = (pair[n, xl] + x_in[n].astype(jnp.float32)).astype(jnp.bfloat16)
            k = n % 8

            @pl.when(k == 0)
            def _():
                fin_in[fin_slot(n)] = done

            @pl.when(k != 0)
            def _():
                fin_out[n] = done
                fin_copy(n, block_z(k)).start()

        return carry

    lax.fori_loop(0, UNITS + 3 * LAG, slot, 0)

    def take(s, carry):
        @pl.when(s % 8 != z)
        def _():
            remote(fin_out.at[0], fin_in.at[s], f_send.at[0], f_recv.at[s], core_peer).wait_recv()
        out_ref[:, pl.ds(pl.multiple_of(s * 768, 128), 768)] = fin_in[s].astype(out_ref.dtype)
        return carry

    lax.fori_loop(0, 16, take, 0)

    for k in range(1, 9):
        block_copy(k).wait_send()
    for n in range(PIECES):
        for way in range(2):
            swap_copy(way, n).wait_send()
            relay_copy(way, n).wait_send()

    def drain(i, carry):
        core_copy(i).wait_send()
        for d in (1, 2, 3):
            y_copy(i, d).wait_send()
        x_copy(i).wait_send()

        @pl.when(i % 8 != 0)
        def _():
            fin_copy(i, block_z(i % 8)).wait_send()
        return carry

    lax.fori_loop(0, UNITS, drain, 0)


def short_call(residual_grad, shortcut):
    bf, f32, dma = jnp.bfloat16, jnp.float32, pltpu.SemaphoreType.DMA
    v = pltpu.VMEM
    return pl.pallas_call(
        short_kernel,
        out_shape=jax.ShapeDtypeStruct((16, 12288), f32),
        in_specs=[pl.BlockSpec(memory_space=pl.ANY)] * 2,
        out_specs=pl.BlockSpec(memory_space=pltpu.VMEM),
        scratch_shapes=[
            v((8, 2, 8, 16, 768), bf), v((2, 768, 768), bf), v((2 * PIECES, 384 // PIECES, 768), bf),
            v((UNITS, 4, 32, 768), bf), v((UNITS, 4, 32, 768), bf), v((UNITS, 4, 32, 768), f32),
            v((UNITS, 4, 32, 768), bf), v((UNITS, 3, 32, 768), bf),
            v((UNITS, 2, 16, 768), f32), v((UNITS, 16, 768), bf), v((UNITS, 16, 768), bf),
            v((UNITS, 16, 768), bf), v((16, 16, 768), bf),
            dma((3,)), dma((9,)), dma((9,)),
            dma((2 * PIECES,)), dma((2 * PIECES,)), dma((2 * PIECES,)), dma((2 * PIECES,)),
            dma((UNITS,)), dma((UNITS,)), dma((UNITS, 3)), dma((UNITS, 3)),
            dma((UNITS,)), dma((UNITS,)), dma((UNITS,)), dma((16,)),
        ],
        compiler_params=pltpu.CompilerParams(
            collective_id=0, has_side_effects=True, vmem_limit_bytes=56 * 1024 * 1024
        ),
        cost_estimate=pl.CostEstimate(flops=4_900_000_000, bytes_accessed=4_000_000, transcendentals=0),
    )(residual_grad.reshape(8, 2, 16, 768), shortcut)
epsilon = 1e-05
adapter_scale = 0.25
HIGH = lax.Precision.HIGHEST


def shards(hidden_in, residual_grad, key_value_gradient, shortcut, key_value_weight, adapter_down_matrix, adapter_up):
    q = lax.axis_index("tensor")
    features = adapter_down_matrix.shape[0]
    inputs = hidden_in.astype(jnp.float32)
    down_rows = lax.dynamic_slice_in_dim(adapter_down_matrix, q * 768, 768, 0)
    sums = jnp.concatenate(
        [
            jnp.dot(inputs, down_rows, precision=HIGH),
            jnp.broadcast_to(jnp.sum(inputs * inputs, axis=1, keepdims=True), (256, 64)),
        ],
        axis=1,
    )
    swapped = lax.ppermute(key_value_weight, ("dp", "tensor"), [(a * 16 + b, b * 16 + a) for a in range(16) for b in range(16)])
    kv_rows = lax.all_gather(swapped, "dp", axis=1, tiled=True)
    kv_all = lax.all_gather(key_value_gradient, "tensor", axis=1, tiled=True)
    sums = lax.psum(sums, "tensor")
    scale = lax.rsqrt(sums[:, 64:65] / features + epsilon)
    low = scale * sums[:, :64]
    back = jnp.dot(kv_all.astype(jnp.float32), adapter_up.T, precision=HIGH)
    normed = inputs * scale
    down_part = adapter_scale * jnp.dot(normed.T, back, precision=HIGH)
    up_part = adapter_scale * jnp.dot(key_value_gradient.astype(jnp.float32).T, low, precision=HIGH)
    shared = lax.psum_scatter(jnp.concatenate([down_part, up_part], axis=0), "dp", scatter_dimension=0, tiled=True)
    grads = lax.all_gather(shared, ("tensor", "dp"), axis=0, tiled=True).reshape(16, 896, 64)
    down_gradient = grads[:, :768].reshape(features, 64)
    up_gradient = grads[:, 768:].reshape(2048, 64).T
    grad_norm = contract(kv_all, kv_rows) + adapter_scale * jnp.dot(back, down_rows.T, precision=HIGH)
    inner = lax.psum(jnp.sum(grad_norm * normed, axis=1, keepdims=True), "tensor") / features
    rest = (scale * (grad_norm - normed * inner)).astype(jnp.bfloat16)
    rest = lax.all_to_all(rest, "tensor", split_axis=0, concat_axis=1, tiled=True)
    short = short_call(residual_grad, shortcut)
    return ((short + rest.astype(jnp.float32)).astype(jnp.bfloat16), down_gradient, up_gradient)


def solution(mesh):
    split = P("dp", "tensor")
    return jax.shard_map(
        shards, mesh=mesh, in_specs=(split,) * 5 + (P(), P()),
        out_specs=(P(("dp", "tensor"), None), P(), P()), check_vma=False,
    )
```

```python
import jax
import jax.numpy as jnp
from jax import lax
from jax.experimental import pallas as pl
from jax.experimental.pallas import tpu as pltpu
from jax.sharding import PartitionSpec as P

MESH = pl.DeviceIdType.MESH
UNITS = 16
LAG = 2
PIECES = 4
epsilon = 1e-05
adapter_scale = 0.25


def place(xh, z, y, xl, c):
    return {"dp": xh * 8 + z, "tensor": (y * 2 + xl) * 2 + c}


def contract(a, b):
    return lax.dot_general(a, b, (((1,), (1,)), ((), ())), preferred_element_type=jnp.float32)


def contract_first(a, b):
    return lax.dot_general(a, b, (((0,), (0,)), ((), ())), preferred_element_type=jnp.float32)


def split(value):
    hi = value.astype(jnp.bfloat16)
    return hi, (value - hi.astype(jnp.float32)).astype(jnp.bfloat16)


def whole_kernel(
    grad_ref, short_ref, hidden_ref, kv_ref, kvw_ref, down_ref, up_ref,
    out_ref, down_out, up_out,
    blocks, weights, relay, core_out, core_in, own, y_out, y_in, pair, x_out, x_in, fin_out, fin_in,
    load_sem, a_send, a_recv, s_send, s_recv, r_send, r_recv,
    core_send, core_recv, y_send, y_recv, x_send, x_recv, f_send, f_recv,
    hidden, hidden_in, kv_all, w_ring, down_rows, up_rows, sums_out, sums_in, sums_all, back_keep,
    norm_sum, norm_out, norm_in, g_out, g_in, g_all,
    h_send, h_recv, k_send, k_recv, su_send, su_recv, sa_send, sa_recv, n_send, n_recv,
    gs_send, gs_recv, gd_send, gd_recv, gt_send, gt_recv, gc_send, gc_recv, t_sem, w_send, w_recv,
):
    p, q = lax.axis_index("dp"), lax.axis_index("tensor")
    xh, z = p // 8, p % 8
    y, xl, c = q // 4, (q // 2) % 2, q % 2
    x = xh * 2 + xl
    xp, xm = (x + 1) % 4, (x + 3) % 4

    def at(xh=xh, z=z, y=y, xl=xl, c=c):
        return place(xh, z, y, xl, c)

    right, left = at(xh=xp // 2, xl=xp % 2), at(xh=xm // 2, xl=xm % 2)
    up, down = at(z=(z + 1) % 8), at(z=(z + 7) % 8)
    core_peer = at(c=1 - c)
    xl_peer = at(xl=1 - xl)

    loads = [pltpu.make_async_copy(grad_ref.at[:, h], blocks.at[0, h], load_sem.at[h]) for h in range(2)]
    loads.append(pltpu.make_async_copy(short_ref, weights.at[0], load_sem.at[2]))
    loads.append(pltpu.make_async_copy(hidden_ref, hidden, load_sem.at[3]))
    loads.append(pltpu.make_async_copy(hidden_ref.at[q], hidden_in.at[q], load_sem.at[4]))
    loads.append(pltpu.make_async_copy(kv_ref, kv_all.at[q], load_sem.at[5]))
    loads.append(
        pltpu.make_async_copy(down_ref.at[pl.ds(pl.multiple_of(q * 768, 768), 768)], down_rows, load_sem.at[6])
    )
    loads.append(pltpu.make_async_copy(up_ref, up_rows, load_sem.at[7]))
    for l in loads:
        l.start()

    barrier = pltpu.get_barrier_semaphore()
    def greet(d, carry):
        pl.semaphore_signal(barrier, inc=1, device_id={"dp": p, "tensor": (q + d) % 16}, device_id_type=MESH)
        pl.semaphore_signal(barrier, inc=1, device_id={"dp": (p + d) % 16, "tensor": q}, device_id_type=MESH)
        return carry

    lax.fori_loop(1, 16, greet, 0)
    pl.semaphore_signal(barrier, inc=1, device_id=at(xh=1 - xh, xl=1 - xl), device_id_type=MESH)

    @pl.when(p != q)
    def _():
        pl.semaphore_signal(barrier, inc=1, device_id={"dp": q, "tensor": p}, device_id_type=MESH)

    for l in loads:
        l.wait()

    @pl.when(p != q)
    def _():
        pl.semaphore_wait(barrier, 32)

    @pl.when(p == q)
    def _():
        pl.semaphore_wait(barrier, 31)

    def remote(src, dst, send, recv, to):
        return pltpu.make_async_remote_copy(
            src_ref=src, dst_ref=dst, send_sem=send, recv_sem=recv, device_id=to, device_id_type=MESH
        )

    rows = 384 // PIECES

    def swap_copy(way, n):
        lo = way * 384 + n * rows
        i = way * PIECES + n
        return remote(
            weights.at[0, pl.ds(lo, rows)], relay.at[i], s_send.at[i], s_recv.at[i], (right, left)[way]
        )

    def relay_copy(way, n):
        lo = way * 384 + n * rows
        i = way * PIECES + n
        return remote(
            relay.at[i], weights.at[1, pl.ds(lo, rows)], r_send.at[i], r_recv.at[i], (right, left)[way]
        )

    def block_copy(k):
        if k == 7:
            return remote(blocks.at[5, 0], blocks.at[7, 0], a_send.at[7], a_recv.at[7], up)
        if k == 8:
            return remote(blocks.at[6, 1], blocks.at[7, 1], a_send.at[8], a_recv.at[8], down)
        source = max(k - 2, 0)
        return remote(blocks.at[source], blocks.at[k], a_send.at[k], a_recv.at[k], up if k % 2 else down)

    block_copy(1).start()
    block_copy(2).start()
    for n in range(PIECES):
        for way in range(2):
            swap_copy(way, n).start()

    def tensor_copy(source, target, send, recv, d):
        return remote(source, target, send.at[d - 1], recv.at[d - 1], {"dp": p, "tensor": (q + d) % 16})

    def dp_copy(source, target, send, recv, d):
        return remote(source, target, send.at[d - 1], recv.at[d - 1], {"dp": (p + d) % 16, "tensor": q})

    def each(body, count=16):
        def step(d, carry):
            body(d)
            return carry
        lax.fori_loop(1, count, step, 0)

    def turn_copy():
        return remote(kvw_ref, w_ring.at[0, q // 8], t_sem.at[0], t_sem.at[1], {"dp": q, "tensor": p})

    def turned():
        return remote(kvw_ref, w_ring.at[0, xh], t_sem.at[0], t_sem.at[1], {"dp": q, "tensor": p})

    def turn_local():
        return pltpu.make_async_copy(kvw_ref, w_ring.at[0, xh], t_sem.at[0])

    def half_copy(which):
        return remote(w_ring.at[0, which], w_ring.at[0, which], t_sem.at[2], t_sem.at[3], at(xh=1 - xh))

    def w_copy(k):
        if k == 7:
            return remote(w_ring.at[5, 0], w_ring.at[7, 0], w_send.at[7], w_recv.at[7], up)
        if k == 8:
            return remote(w_ring.at[6, 1], w_ring.at[7, 1], w_send.at[8], w_recv.at[8], down)
        return remote(w_ring.at[max(k - 2, 0)], w_ring.at[k], w_send.at[k], w_recv.at[k], up if k % 2 else down)

    @pl.when(p != q)
    def _():
        turn_copy().start()

    @pl.when(p == q)
    def _():
        turn_local().start()

    down_hi, down_lo = split(down_rows[...])
    local = hidden[...].reshape(256, 768)
    low = jnp.dot(local, jnp.concatenate([down_hi, down_lo], axis=1), preferred_element_type=jnp.float32)
    wide = local.astype(jnp.float32)
    squares = jnp.sum(wide * wide, axis=1, keepdims=True)
    sums = jnp.concatenate([low[:, :64] + low[:, 64:], jnp.broadcast_to(squares, (256, 64))], axis=1)
    sums_out[...] = sums.reshape(16, 16, 128)
    each(lambda d: tensor_copy(sums_out.at[(q + d) % 16], sums_in.at[q], su_send, su_recv, d).start())
    sums_in[q] = sums_out[q]
    each(lambda d: tensor_copy(kv_ref, kv_all.at[q], k_send, k_recv, d).start())
    each(lambda d: tensor_copy(hidden_ref.at[(q + d) % 16], hidden_in.at[q], h_send, h_recv, d).start())

    def sums_reduce():
        each(lambda d: tensor_copy(sums_out.at[0], sums_in.at[(q + 16 - d) % 16], su_send, su_recv, d).wait_recv())
        sums_all[q] = jnp.sum(sums_in[...], axis=0)
        each(lambda d: tensor_copy(sums_all.at[q], sums_all.at[q], sa_send, sa_recv, d).start())

    def adapter_parts():
        each(lambda d: tensor_copy(sums_out.at[0], sums_all.at[(q + 16 - d) % 16], sa_send, sa_recv, d).wait_recv())
        each(lambda d: tensor_copy(kv_ref, kv_all.at[(q + 16 - d) % 16], k_send, k_recv, d).wait_recv())

        def add(s, total):
            hi, lo = split(up_rows[:, pl.ds(pl.multiple_of(s * 128, 128), 128)])
            return total + contract(kv_all[s], jnp.concatenate([hi, lo], axis=0))

        both = lax.fori_loop(0, 16, add, jnp.zeros((256, 128), jnp.float32))
        back = both[:, :64] + both[:, 64:]
        back_keep[...] = back
        reduced = sums_all[...].reshape(256, 128)
        scale = lax.rsqrt(reduced[:, 64:65] / 12288 + epsilon)
        low = jnp.concatenate(split(scale * reduced[:, :64]), axis=1)
        upper = contract_first(low, kv_all[q])
        g_out[...] = jnp.zeros_like(g_out)
        g_out[0:8, 24:32] = (adapter_scale * (upper[:64] + upper[64:])).reshape(8, 8, 128)
        scaled = jnp.concatenate(split(scale * back), axis=1)
        lower = contract_first(hidden[...].reshape(256, 768), scaled)
        lower = adapter_scale * (lower[:, :64] + lower[:, 64:])
        g_out[:, 0:24] = jnp.concatenate([lower[:384], lower[384:]], axis=1).reshape(16, 24, 128)
        each(lambda d: dp_copy(g_out.at[(p + d) % 16], g_in.at[p], gs_send, gs_recv, d).start())
        g_in[p] = g_out[p]

    def grads_reduce():
        each(lambda d: dp_copy(g_out.at[0], g_in.at[(p + 16 - d) % 16], gs_send, gs_recv, d).wait_recv())
        g_all[q, p] = jnp.sum(g_in[...], axis=0).astype(jnp.bfloat16)
        each(lambda d: dp_copy(g_all.at[q, p], g_all.at[q, p], gd_send, gd_recv, d).start())

    def chips_copy(s, e):
        return remote(
            g_all.at[s], g_all.at[s], gt_send.at[e - 1], gt_recv.at[e - 1], {"dp": p, "tensor": (q + 2 * e) % 16}
        )

    def other_core_copy(s, e):
        return remote(g_all.at[s], g_all.at[s], gc_send.at[e], gc_recv.at[e], core_peer)

    def grads_spread():
        each(lambda d: dp_copy(g_all.at[0, 0], g_all.at[q, (p + 16 - d) % 16], gd_send, gd_recv, d).wait_recv())
        each(lambda e: chips_copy(q, e).start(), 8)
        other_core_copy(q, 0).start()

    def grads_forward():
        def body(e):
            s = (q + 16 - 2 * e) % 16
            chips_copy(s, e).wait_recv()
            other_core_copy(s, e).start()
        each(body, 8)

    def norm_add(k, first=False):
        z_from = block_z(k)
        term = contract(kv_all[z_from], w_ring[k, 0]) + contract(kv_all[8 + z_from], w_ring[k, 1])
        norm_sum[...] = term if first else norm_sum[...] + term

    def norm_begin():
        half_copy(1 - xh).wait_recv()
        w_copy(1).start()
        w_copy(2).start()
        norm_add(0, True)
        back_hi, back_lo = split(back_keep[...])
        down_hi, down_lo = split(down_rows[...])
        extra = contract(
            jnp.concatenate([back_hi, back_lo], axis=1), jnp.concatenate([down_hi, down_hi], axis=1)
        ) + contract(back_hi, down_lo)
        norm_sum[...] += adapter_scale * extra

    def norm_hop(first, second):
        for k in (first, second):
            w_copy(k).wait_recv()
            if k < 7:
                w_copy(k + 2).start()
        for k in ((first, second) if first < 7 else (7,)):
            norm_add(k)

    def norm_send():
        norm_out[...] = norm_sum[...].astype(jnp.bfloat16).reshape(16, 16, 768)
        each(lambda d: tensor_copy(norm_out.at[(q + d) % 16], norm_in.at[q], n_send, n_recv, d).start())
        norm_in[q] = norm_out[q]

    def turn_done():
        @pl.when(p != q)
        def _():
            turned().wait_recv()

        @pl.when(p == q)
        def _():
            turn_local().wait()

        half_copy(xh).start()

    def core_copy(i):
        return remote(core_out.at[i], core_in.at[i], core_send.at[i], core_recv.at[i], core_peer)

    def y_copy(i, d):
        to = (y + d) % 4
        return remote(y_out.at[i, to], y_in.at[i, d - 1], y_send.at[i, d - 1], y_recv.at[i, d - 1], at(y=to))

    def x_copy(i):
        return remote(x_out.at[i], x_in.at[i], x_send.at[i], x_recv.at[i], xl_peer)

    def fin_slot(i):
        g = i // 8
        return (xh + g - 2 * xh * g) * 8 + z

    def fin_copy(i, to_z):
        s = fin_slot(i)
        return remote(fin_out.at[i], fin_in.at[s], f_send.at[i], f_recv.at[s], at(z=to_z))

    def block_z(k):
        half = (k + 1) // 2
        return lax.rem(z + 8 + half - 2 * half * (k % 2), 8)

    plan = {
        2: [turn_done], 3: [sums_reduce], 5: [adapter_parts], 7: [grads_reduce, norm_begin], 9: [grads_spread],
        10: [lambda: norm_hop(1, 2)], 13: [lambda: norm_hop(3, 4)], 14: [grads_forward],
        16: [lambda: norm_hop(5, 6)], 19: [lambda: norm_hop(7, 8), norm_send],
    }

    def slot(i, carry):
        for k in range(1, 8):
            @pl.when(i == k)
            def _():
                block_copy(k).wait_recv()
                if k == 7:
                    block_copy(8).wait_recv()
                if k <= 4:
                    block_copy(k + 2).start()
                elif k <= 6:
                    block_copy(k + 2).start()
                if 1 <= k <= PIECES:
                    for way in range(2):
                        swap_copy(way, k - 1).wait_recv()
                        relay_copy(way, k - 1).start()

        @pl.when(i == 8)
        def _():
            for n in range(PIECES):
                for way in range(2):
                    relay_copy(way, n).wait_recv()

        @pl.when(i < UNITS)
        def _():
            k, g = i % 8, i // 8
            theirs = contract(blocks[k, 1 - c].reshape(128, 768), weights[g])
            core_out[i] = theirs.astype(jnp.bfloat16).reshape(4, 32, 768)
            core_copy(i).start()
            own[i] = contract(blocks[k, c].reshape(128, 768), weights[g]).reshape(4, 32, 768)

        for when, acts in plan.items():
            @pl.when(i == when)
            def _(acts=acts):
                for act in acts:
                    act()

        j = i - LAG

        @pl.when(jnp.logical_and(j >= 0, j < UNITS))
        def _():
            core_copy(j).wait_recv()
            total = own[j] + core_in[j].astype(jnp.float32)
            own[j] = total
            y_out[j] = total.astype(jnp.bfloat16)
            for d in (2, 1, 3):
                y_copy(j, d).start()

        m = i - 2 * LAG

        @pl.when(jnp.logical_and(m >= 0, m < UNITS))
        def _():
            for d in (1, 2, 3):
                y_copy(m, d).wait_recv()
            got = y_in[m].astype(jnp.float32)
            total = ((own[m, y] + got[0]) + (got[1] + got[2])).reshape(2, 16, 768)
            pair[m] = total
            x_out[m] = pair[m, 1 - xl].astype(jnp.bfloat16)
            x_copy(m).start()

        n = i - 3 * LAG

        @pl.when(jnp.logical_and(n >= 0, n < UNITS))
        def _():
            x_copy(n).wait_recv()
            done = (pair[n, xl] + x_in[n].astype(jnp.float32)).astype(jnp.bfloat16)
            k = n % 8

            @pl.when(k == 0)
            def _():
                fin_in[fin_slot(n)] = done

            @pl.when(k != 0)
            def _():
                fin_out[n] = done
                fin_copy(n, block_z(k)).start()

        return carry

    lax.fori_loop(0, UNITS + 3 * LAG, slot, 0)

    each(lambda e: other_core_copy((q + 1 - 2 * c + 16 - 2 * e) % 16, e).wait_recv(), 8)
    other_core_copy(q + 1 - 2 * c, 0).wait_recv()

    def unpack(s, carry):
        packed = g_all[s].astype(jnp.float32)
        lower = packed[:, :24].reshape(384, 128)
        first = pl.multiple_of(s * 768, 128)
        down_out[pl.ds(first, 384)] = lower[:, :64].astype(down_out.dtype)
        down_out[pl.ds(first + 384, 384)] = lower[:, 64:].astype(down_out.dtype)
        up_out[:, pl.ds(pl.multiple_of(s * 128, 128), 128)] = packed[:8, 24:].reshape(64, 128).astype(up_out.dtype)
        return carry

    lax.fori_loop(0, 16, unpack, 0)

    each(lambda d: tensor_copy(kv_ref, hidden_in.at[(q + 16 - d) % 16], h_send, h_recv, d).wait_recv())
    each(lambda d: tensor_copy(norm_out.at[0], norm_in.at[(q + 16 - d) % 16], n_send, n_recv, d).wait_recv())
    my_scale = lax.rsqrt(sums_all[q][:, 64:65] / 12288 + epsilon)

    def dots(s, total):
        return total + hidden_in[s].astype(jnp.float32) * norm_in[s].astype(jnp.float32)

    products = lax.fori_loop(0, 16, dots, jnp.zeros((16, 768), jnp.float32))
    inner = jnp.sum(products, axis=1, keepdims=True) * my_scale / 12288

    def take(s, carry):
        @pl.when(s % 8 != z)
        def _():
            remote(fin_out.at[0], fin_in.at[s], f_send.at[0], f_recv.at[s], core_peer).wait_recv()
        normed = hidden_in[s].astype(jnp.float32) * my_scale
        done = fin_in[s].astype(jnp.float32) + my_scale * (norm_in[s].astype(jnp.float32) - normed * inner)
        out_ref[:, pl.ds(pl.multiple_of(s * 768, 128), 768)] = done.astype(out_ref.dtype)
        return carry

    lax.fori_loop(0, 16, take, 0)

    for k in range(1, 9):
        block_copy(k).wait_send()
    for n in range(PIECES):
        for way in range(2):
            swap_copy(way, n).wait_send()
            relay_copy(way, n).wait_send()

    def drain(i, carry):
        core_copy(i).wait_send()
        for d in (1, 2, 3):
            y_copy(i, d).wait_send()
        x_copy(i).wait_send()

        @pl.when(i % 8 != 0)
        def _():
            fin_copy(i, block_z(i % 8)).wait_send()
        return carry

    lax.fori_loop(0, UNITS, drain, 0)
    for k in range(1, 9):
        w_copy(k).wait_send()
    half_copy(xh).wait_send()

    @pl.when(p != q)
    def _():
        turn_copy().wait_send()

    def drain_all(d):
        tensor_copy(sums_out.at[(q + d) % 16], sums_in.at[q], su_send, su_recv, d).wait_send()
        tensor_copy(sums_all.at[q], sums_all.at[q], sa_send, sa_recv, d).wait_send()
        tensor_copy(kv_ref, kv_all.at[q], k_send, k_recv, d).wait_send()
        tensor_copy(hidden_ref.at[(q + d) % 16], hidden_in.at[q], h_send, h_recv, d).wait_send()
        tensor_copy(norm_out.at[(q + d) % 16], norm_in.at[q], n_send, n_recv, d).wait_send()
        dp_copy(g_out.at[(p + d) % 16], g_in.at[p], gs_send, gs_recv, d).wait_send()
        dp_copy(g_all.at[q, p], g_all.at[q, p], gd_send, gd_recv, d).wait_send()

    each(drain_all)
    other_core_copy(q, 0).wait_send()

    def drain_grads(e):
        chips_copy(q, e).wait_send()
        other_core_copy((q + 16 - 2 * e) % 16, e).wait_send()

    each(drain_grads, 8)


def shards(hidden_in, residual_grad, key_value_gradient, shortcut, key_value_weight, adapter_down_matrix, adapter_up):
    bf, f32, dma = jnp.bfloat16, jnp.float32, pltpu.SemaphoreType.DMA
    v = pltpu.VMEM
    result, down, up = pl.pallas_call(
        whole_kernel,
        out_shape=[
            jax.ShapeDtypeStruct((16, 12288), bf),
            jax.ShapeDtypeStruct((12288, 64), bf),
            jax.ShapeDtypeStruct((64, 2048), bf),
        ],
        in_specs=[pl.BlockSpec(memory_space=pl.ANY)] * 7,
        out_specs=[pl.BlockSpec(memory_space=pltpu.VMEM)] * 3,
        scratch_shapes=[
            v((8, 2, 8, 16, 768), bf), v((2, 768, 768), bf), v((2 * PIECES, 384 // PIECES, 768), bf),
            v((UNITS, 4, 32, 768), bf), v((UNITS, 4, 32, 768), bf), v((UNITS, 4, 32, 768), f32),
            v((UNITS, 4, 32, 768), bf), v((UNITS, 3, 32, 768), bf),
            v((UNITS, 2, 16, 768), f32), v((UNITS, 16, 768), bf), v((UNITS, 16, 768), bf),
            v((UNITS, 16, 768), bf), v((16, 16, 768), bf),
            dma((8,)), dma((9,)), dma((9,)),
            dma((2 * PIECES,)), dma((2 * PIECES,)), dma((2 * PIECES,)), dma((2 * PIECES,)),
            dma((UNITS,)), dma((UNITS,)), dma((UNITS, 3)), dma((UNITS, 3)),
            dma((UNITS,)), dma((UNITS,)), dma((UNITS,)), dma((16,)),
            v((16, 16, 768), bf), v((16, 16, 768), bf), v((16, 256, 128), bf), v((8, 2, 768, 128), bf),
            v((768, 64), f32), v((64, 2048), f32), v((16, 16, 128), f32), v((16, 16, 128), f32),
            v((16, 16, 128), f32), v((256, 64), f32),
            v((256, 768), f32), v((16, 16, 768), bf), v((16, 16, 768), bf),
            v((16, 32, 128), f32), v((16, 32, 128), f32), v((16, 16, 32, 128), bf),
            *[dma((15,))] * 10, *[dma((15,))] * 4, dma((7,)), dma((7,)), dma((8,)), dma((8,)),
            dma((4,)), dma((9,)), dma((9,)),
        ],
        compiler_params=pltpu.CompilerParams(
            collective_id=0, has_side_effects=True, vmem_limit_bytes=58 * 1024 * 1024
        ),
        cost_estimate=pl.CostEstimate(flops=5_900_000_000, bytes_accessed=12_000_000, transcendentals=512),
    )(
        residual_grad.reshape(8, 2, 16, 768), shortcut, hidden_in.reshape(16, 16, 768), key_value_gradient, key_value_weight,
        adapter_down_matrix, adapter_up,
    )
    return result, down.astype(f32), up.astype(f32)


def solution(mesh):
    part = P("dp", "tensor")
    return jax.shard_map(
        shards, mesh=mesh, in_specs=(part,) * 5 + (P(), P()),
        out_specs=(P(("dp", "tensor"), None), P(), P()), check_vma=False,
    )
```

```python
import jax
import jax.numpy as jnp
from jax import lax
from jax.experimental import pallas as pl
from jax.experimental.pallas import tpu as pltpu
from jax.sharding import PartitionSpec as P

MESH = pl.DeviceIdType.MESH
UNITS = 8
LAGS = (1, 2, 3, 4)
epsilon = 1e-05
adapter_scale = 0.25


def place(xh, z, y, xl, c):
    return {"dp": xh * 8 + z, "tensor": (y * 2 + xl) * 2 + c}


def contract(a, b):
    return lax.dot_general(a, b, (((1,), (1,)), ((), ())), preferred_element_type=jnp.float32)


def multiply(a, b):
    return jnp.dot(a, b, preferred_element_type=jnp.float32)


def contract_first(a, b):
    return lax.dot_general(a, b, (((0,), (0,)), ((), ())), preferred_element_type=jnp.float32)


def split(value):
    hi = value.astype(jnp.bfloat16)
    return hi, (value - hi.astype(jnp.float32)).astype(jnp.bfloat16)


def whole_kernel(
    grad_ref, short_ref, hidden_ref, kv_ref, kvw_ref, down_ref, up_ref,
    out_ref, down_out, up_out,
    blocks, weights, core_out, core_in, own, y_out, far_in, y_in, pair, x_out, x_in, fin_out, fin_in,
    hidden, hidden_in, kv_all, w_ring, down_rows, up_rows, sums_out, sums_in, sums_all, back_keep,
    norm_sum, norm_out, norm_in, g_out, g_in, g_all, g_rows,
    load_sem, a_send, a_recv, s_sem,
    core_send, core_recv, far_send, far_recv, near_send, near_recv, x_send, x_recv, f_sem,
    h_sem, k_sem, su_sem, sa_sem, n_sem, gs_sem, gd_sem, gt_send, gt_recv, gc_sem, t_sem, w_send, w_recv,
):
    p, q = lax.axis_index("dp"), lax.axis_index("tensor")
    xh, z = p // 8, p % 8
    y, xl, c = q // 4, (q // 2) % 2, q % 2

    def at(xh=xh, z=z, y=y, xl=xl, c=c):
        return place(xh, z, y, xl, c)

    up, down = at(z=(z + 1) % 8), at(z=(z + 7) % 8)
    core_peer = at(c=1 - c)
    xl_peer = at(xl=1 - xl)

    def local(source, target, i):
        return pltpu.make_async_copy(source, target, load_sem.at[i])

    loads = [local(grad_ref.at[:, h], blocks.at[7, h], h) for h in range(2)]
    loads.append(local(short_ref, weights.at[0], 2))
    loads.append(local(hidden_ref, hidden, 3))
    loads.append(local(hidden_ref.at[q], hidden_in.at[q], 4))
    loads.append(local(kv_ref, kv_all.at[q], 5))
    loads.append(local(down_ref.at[:, pl.ds(pl.multiple_of(q * 768, 128), 768)], down_rows, 6))
    loads.append(local(up_ref, up_rows, 7))
    for l in loads:
        l.start()

    barrier = pltpu.get_barrier_semaphore()

    def each(body, count=16):
        def step(d, carry):
            body(d)
            return carry
        lax.fori_loop(1, count, step, 0)

    def turn(a, d):
        return lax.rem(a + d, 16)

    def greet(d):
        pl.semaphore_signal(barrier, inc=1, device_id={"dp": p, "tensor": turn(q, d)}, device_id_type=MESH)
        pl.semaphore_signal(barrier, inc=1, device_id={"dp": turn(p, d), "tensor": q}, device_id_type=MESH)

    each(greet)

    @pl.when(p != q)
    def _():
        pl.semaphore_signal(barrier, inc=1, device_id={"dp": q, "tensor": p}, device_id_type=MESH)

    for l in loads:
        l.wait()

    @pl.when(p != q)
    def _():
        pl.semaphore_wait(barrier, 31)

    @pl.when(p == q)
    def _():
        pl.semaphore_wait(barrier, 30)

    def remote(src, dst, send, recv, to):
        return pltpu.make_async_remote_copy(
            src_ref=src, dst_ref=dst, send_sem=send, recv_sem=recv, device_id=to, device_id_type=MESH
        )

    def group(ref, sems):
        return remote(ref, ref, sems.at[0], sems.at[1], core_peer)

    def ring_copy(buffer, send, recv, s, h):
        source = 7 if s < 2 else (4 + h if s == 6 else s - 2)
        way = (up, down)[h if s == 6 else s % 2]
        return remote(buffer.at[source, h], buffer.at[s, h], send.at[0], recv.at[s, h], way)

    def block_copy(s, h):
        return ring_copy(blocks, a_send, a_recv, s, h)

    def w_copy(s, h):
        return ring_copy(w_ring, w_send, w_recv, s, h)

    def ring_step(copy, t):
        if t == 3:
            copy(6, 0).wait_recv()
            copy(6, 1).wait_recv()
            return
        for h in range(2):
            for s in (2 * t, 2 * t + 1):
                copy(s, h).wait_recv()
                if s < 4:
                    copy(s + 2, h).start()
                elif s - 4 == h:
                    copy(6, h).start()

    for h in range(2):
        for s in range(2):
            block_copy(s, h).start()

    def swap_copy():
        return remote(weights.at[0], weights.at[1], s_sem.at[0], s_sem.at[1], at(xh=1 - xh))

    swap_copy().start()

    def to_tensor(source, target, sems, d):
        return remote(source, target, sems.at[0], sems.at[1], {"dp": p, "tensor": turn(q, d)})

    def to_dp(source, target, sems, d):
        return remote(source, target, sems.at[0], sems.at[1], {"dp": turn(p, d), "tensor": q})

    def turn_copy(part):
        return remote(kvw_ref, w_ring.at[7, part], t_sem.at[0], t_sem.at[1], {"dp": q, "tensor": p})

    def turn_local():
        return pltpu.make_async_copy(kvw_ref, w_ring.at[7, xh], t_sem.at[0])

    def half_copy(part):
        return remote(w_ring.at[7, part], w_ring.at[7, part], t_sem.at[2], t_sem.at[3], at(xh=1 - xh))

    @pl.when(p != q)
    def _():
        turn_copy(q // 8).start()

    @pl.when(p == q)
    def _():
        turn_local().start()

    down_hi, down_lo = split(down_rows[...])
    mine = hidden[...].reshape(256, 768)
    low = contract(mine, jnp.concatenate([down_hi, down_lo], axis=0))
    wide = mine.astype(jnp.float32)
    squares = jnp.sum(wide * wide, axis=1, keepdims=True)
    sums = jnp.concatenate([low[:, :64] + low[:, 64:], jnp.broadcast_to(squares, (256, 64))], axis=1)
    sums_out[...] = sums.reshape(16, 16, 128)
    each(lambda d: to_tensor(sums_out.at[turn(q, d)], sums_in.at[q], su_sem, d).start())
    sums_in[q] = sums_out[q]
    each(lambda d: to_tensor(kv_ref, kv_all.at[q], k_sem, d).start())
    each(lambda d: to_tensor(hidden_ref.at[turn(q, d)], hidden_in.at[q], h_sem, d).start())

    def sums_reduce():
        group(sums_in.at[pl.ds(0, 15)], su_sem).wait_recv()
        sums_all[q] = jnp.sum(sums_in[...], axis=0)
        each(lambda d: to_tensor(sums_all.at[q], sums_all.at[q], sa_sem, d).start())

    def adapter_parts():
        group(sums_all.at[pl.ds(0, 15)], sa_sem).wait_recv()
        group(kv_all.at[pl.ds(0, 15)], k_sem).wait_recv()
        both = jnp.zeros((256, 128), jnp.float32)
        for s in range(16):
            hi, lo = split(up_rows[:, 128 * s : 128 * s + 128])
            both = both + contract(kv_all[s], jnp.concatenate([hi, lo], axis=0))
        back = both[:, :64] + both[:, 64:]
        back_keep[...] = back
        reduced = sums_all[...].reshape(256, 128)
        scale = lax.rsqrt(reduced[:, 64:65] / 12288 + epsilon)
        low = jnp.concatenate(split(scale * reduced[:, :64]), axis=1)
        upper = contract_first(low, kv_all[q])
        g_out[8:16, 24:32] = jnp.zeros((8, 8, 128), jnp.float32)
        g_out[0:8, 24:32] = (adapter_scale * (upper[:64] + upper[64:])).reshape(8, 8, 128)
        scaled = jnp.concatenate(split(scale * back), axis=1)
        lower = contract_first(scaled, hidden[...].reshape(256, 768))
        lower = adapter_scale * (lower[:64] + lower[64:])
        for b in range(6):
            g_rows[64 * b : 64 * b + 64] = lower[:, 128 * b : 128 * b + 128]
        g_out[:, 0:24] = g_rows[...].reshape(16, 24, 128)
        each(lambda d: to_dp(g_out.at[turn(p, d)], g_in.at[p], gs_sem, d).start())
        g_in[p] = g_out[p]

    def grads_reduce():
        group(g_in.at[pl.ds(0, 15)], gs_sem).wait_recv()
        g_all[q, p] = jnp.sum(g_in[...], axis=0).astype(jnp.bfloat16)
        each(lambda d: to_dp(g_all.at[q, p], g_all.at[q, p], gd_sem, d).start())

    def chips_copy(s, e):
        return remote(
            g_all.at[s], g_all.at[s], gt_send.at[0], gt_recv.at[e - 1], {"dp": p, "tensor": turn(q, 2 * e)}
        )

    def other_core_copy(s):
        return remote(g_all.at[s], g_all.at[s], gc_sem.at[0], gc_sem.at[1], core_peer)

    def grads_spread():
        group(g_all.at[q, pl.ds(0, 15)], gd_sem).wait_recv()
        each(lambda e: chips_copy(q, e).start(), 8)
        other_core_copy(q).start()

    def grads_forward():
        def body(e):
            s = turn(q, 16 - 2 * e)
            chips_copy(s, e).wait_recv()
            other_core_copy(s).start()
        each(body, 8)

    def block_z(s):
        half = (s + 2) // 2
        return lax.rem(z + 8 + jnp.where(s == 7, 0, jnp.where(s % 2 == 0, -half, half)), 8)

    def norm_term(slots):
        left = [kv_all[8 * part + block_z(s)] for s in slots for part in range(2)]
        right = [w_ring[s, part] for s in slots for part in range(2)]
        return contract(jnp.concatenate(left, axis=1), jnp.concatenate(right, axis=1))

    def norm_begin():
        half_copy(1 - xh).wait_recv()
        for h in range(2):
            for s in range(2):
                w_copy(s, h).start()

    def norm_hop(t):
        ring_step(w_copy, t)
        term = norm_term((2 * t, 2 * t + 1))
        norm_sum[...] = term if t == 0 else norm_sum[...] + term

    def norm_send():
        back_hi, back_lo = split(back_keep[...])
        down_hi, down_lo = split(down_rows[...])
        extra = multiply(
            jnp.concatenate([back_hi, back_lo], axis=1), jnp.concatenate([down_hi, down_hi], axis=0)
        ) + multiply(back_hi, down_lo)
        total = norm_sum[...] + adapter_scale * extra
        norm_out[...] = total.astype(jnp.bfloat16).reshape(16, 16, 768)
        each(lambda d: to_tensor(norm_out.at[turn(q, d)], norm_in.at[q], n_sem, d).start())
        norm_in[q] = norm_out[q]

    def turn_done():
        @pl.when(p != q)
        def _():
            turn_copy(xh).wait_recv()

        @pl.when(p == q)
        def _():
            turn_local().wait()

        half_copy(xh).start()

    def core_copy(i):
        return remote(core_out.at[i], core_in.at[i], core_send.at[0], core_recv.at[i], core_peer)

    def far_copy(i, way):
        return remote(
            y_out.at[i, (y + 2) % 4, way], far_in.at[i, way], far_send.at[0], far_recv.at[i, way],
            at(y=(y + 1 + 2 * way) % 4),
        )

    def near_copy(i, way):
        to = (y + 1 + 2 * way) % 4
        return remote(y_out.at[i, to], y_in.at[i, way], near_send.at[0], near_recv.at[i, way], at(y=to))

    def x_copy(i):
        return remote(x_out.at[i], x_in.at[i], x_send.at[0], x_recv.at[i], xl_peer)

    def fin_slot(i):
        g = i // 4
        return (xh + g - 2 * xh * g) * 8 + z

    before = {
        0: [lambda: ring_step(block_copy, 0)],
        1: [lambda: ring_step(block_copy, 1)],
        2: [lambda: ring_step(block_copy, 2)],
        3: [lambda: ring_step(block_copy, 3)],
        4: [lambda: swap_copy().wait_recv()],
    }
    after = {
        0: [turn_done],
        2: [norm_begin, sums_reduce],
        4: [adapter_parts],
        5: [lambda: norm_hop(0)],
        6: [grads_reduce],
        7: [lambda: norm_hop(1)],
        8: [grads_spread],
        9: [lambda: norm_hop(2)],
        10: [grads_forward],
        11: [lambda: norm_hop(3), norm_send],
    }

    def run(table, i):
        for when, acts in table.items():
            @pl.when(i == when)
            def _(acts=acts):
                for act in acts:
                    act()

    def step(i, carry):
        run(before, i)

        @pl.when(i < UNITS)
        def _():
            t, g = i % 4, i // 4
            both = contract(blocks[pl.ds(2 * t, 2)].reshape(512, 768), weights[g]).reshape(2, 2, 4, 32, 768)
            first, second = both[:, 0], both[:, 1]
            theirs = jnp.where(c == 0, second, first).astype(jnp.bfloat16)
            mine = jnp.where(c == 0, first, second)
            for b in range(2):
                core_out[i, :, b] = theirs[b]
            core_copy(i).start()
            for b in range(2):
                own[i, :, b] = mine[b]

        j = i - LAGS[0]

        @pl.when(jnp.logical_and(j >= 0, j < UNITS))
        def _():
            core_copy(j).wait_recv()
            total = own[j] + core_in[j].astype(jnp.float32)
            own[j] = total
            y_out[j] = total.astype(jnp.bfloat16)
            far_copy(j, 0).start()
            far_copy(j, 1).start()

        r = i - LAGS[1]

        @pl.when(jnp.logical_and(r >= 0, r < UNITS))
        def _():
            for way in range(2):
                far_copy(r, way).wait_recv()
                to = (y + 1 + 2 * way) % 4
                y_out[r, to, way] = (own[r, to, way] + far_in[r, way].astype(jnp.float32)).astype(jnp.bfloat16)
                near_copy(r, way).start()

        m = i - LAGS[2]

        @pl.when(jnp.logical_and(m >= 0, m < UNITS))
        def _():
            for way in range(2):
                near_copy(m, way).wait_recv()
            got = y_in[m].astype(jnp.float32)
            total = (own[m, y] + (got[0] + got[1])).reshape(2, 2, 16, 768)
            pair[m] = total
            for b in range(2):
                x_out[m, b] = pair[m, b, 1 - xl].astype(jnp.bfloat16)
            x_copy(m).start()

        n = i - LAGS[3]

        @pl.when(jnp.logical_and(n >= 0, n < UNITS))
        def _():
            x_copy(n).wait_recv()
            for b in range(2):
                done = (pair[n, b, xl] + x_in[n, b].astype(jnp.float32)).astype(jnp.bfloat16)
                s = 2 * (n % 4) + b
                slot = fin_slot(n)

                @pl.when(s == 7)
                def _():
                    fin_in[slot] = done

                @pl.when(s != 7)
                def _():
                    fin_out[n, b] = done
                    remote(
                        fin_out.at[n, b], fin_in.at[slot], f_sem.at[0], f_sem.at[1], at(z=block_z(s))
                    ).start()

        run(after, i)
        return carry

    lax.fori_loop(0, UNITS + LAGS[3], step, 0)

    group(g_all.at[pl.ds(0, 8)], gc_sem).wait_recv()

    def unpack(s, carry):
        packed = g_all[s].astype(jnp.float32)
        lower = packed[:, :24].reshape(6, 64, 128)
        for b in range(6):
            down_out[:, pl.ds(pl.multiple_of(s * 768 + 128 * b, 128), 128)] = lower[b].astype(down_out.dtype)
        up_out[:, pl.ds(pl.multiple_of(s * 128, 128), 128)] = packed[:8, 24:].reshape(64, 128).astype(up_out.dtype)
        return carry

    lax.fori_loop(0, 16, unpack, 0)

    group(hidden_in.at[pl.ds(0, 15)], h_sem).wait_recv()
    group(norm_in.at[pl.ds(0, 15)], n_sem).wait_recv()
    my_scale = lax.rsqrt(sums_all[q][:, 64:65] / 12288 + epsilon)

    def dots(s, total):
        return total + hidden_in[s].astype(jnp.float32) * norm_in[s].astype(jnp.float32)

    products = lax.fori_loop(0, 16, dots, jnp.zeros((16, 768), jnp.float32))
    inner = jnp.sum(products, axis=1, keepdims=True) * my_scale / 12288
    group(fin_in.at[pl.ds(0, 14)], f_sem).wait_recv()

    def take(s, carry):
        normed = hidden_in[s].astype(jnp.float32) * my_scale
        done = fin_in[s].astype(jnp.float32) + my_scale * (norm_in[s].astype(jnp.float32) - normed * inner)
        out_ref[:, pl.ds(pl.multiple_of(s * 768, 128), 768)] = done.astype(out_ref.dtype)
        return carry

    lax.fori_loop(0, 16, take, 0)

    def gone(ref, sems):
        remote(ref, ref, sems.at[0], sems.at[0], core_peer).wait_send()

    gone(blocks.at[pl.ds(0, 7)], a_send)
    gone(w_ring.at[pl.ds(0, 7)], w_send)
    swap_copy().wait_send()
    gone(core_out, core_send)
    gone(far_in, far_send)
    gone(y_in, near_send)
    gone(x_out, x_send)
    gone(fin_in.at[pl.ds(0, 14)], f_sem)
    half_copy(xh).wait_send()

    @pl.when(p != q)
    def _():
        turn_copy(q // 8).wait_send()

    gone(sums_in.at[pl.ds(0, 15)], su_sem)
    gone(sums_all.at[pl.ds(0, 15)], sa_sem)
    gone(kv_all.at[pl.ds(0, 15)], k_sem)
    gone(hidden_in.at[pl.ds(0, 15)], h_sem)
    gone(norm_in.at[pl.ds(0, 15)], n_sem)
    gone(g_in.at[pl.ds(0, 15)], gs_sem)
    gone(g_all.at[0, pl.ds(0, 15)], gd_sem)
    gone(g_all.at[pl.ds(0, 7)], gt_send)
    gone(g_all.at[pl.ds(0, 8)], gc_sem)


def shards(hidden_in, residual_grad, key_value_gradient, shortcut, key_value_weight, adapter_down_matrix, adapter_up):
    bf, f32, dma = jnp.bfloat16, jnp.float32, pltpu.SemaphoreType.DMA
    v = pltpu.VMEM
    result, down, up = pl.pallas_call(
        whole_kernel,
        out_shape=[
            jax.ShapeDtypeStruct((16, 12288), bf),
            jax.ShapeDtypeStruct((64, 12288), bf),
            jax.ShapeDtypeStruct((64, 2048), bf),
        ],
        in_specs=[pl.BlockSpec(memory_space=pl.ANY)] * 7,
        out_specs=[pl.BlockSpec(memory_space=pltpu.VMEM)] * 3,
        scratch_shapes=[
            v((8, 2, 8, 16, 768), bf), v((2, 768, 768), bf),
            v((UNITS, 4, 2, 32, 768), bf), v((UNITS, 4, 2, 32, 768), bf), v((UNITS, 4, 2, 32, 768), f32),
            v((UNITS, 4, 2, 32, 768), bf), v((UNITS, 2, 32, 768), bf), v((UNITS, 2, 2, 32, 768), bf),
            v((UNITS, 2, 2, 16, 768), f32), v((UNITS, 2, 16, 768), bf), v((UNITS, 2, 16, 768), bf),
            v((UNITS, 2, 16, 768), bf), v((16, 16, 768), bf),
            v((16, 16, 768), bf), v((16, 16, 768), bf), v((16, 256, 128), bf), v((8, 2, 768, 128), bf),
            v((64, 768), f32), v((64, 2048), f32), v((16, 16, 128), f32), v((16, 16, 128), f32),
            v((16, 16, 128), f32), v((256, 64), f32),
            v((256, 768), f32), v((16, 16, 768), bf), v((16, 16, 768), bf),
            v((16, 32, 128), f32), v((16, 32, 128), f32), v((16, 16, 32, 128), bf), v((384, 128), f32),
            dma((8,)), dma((1,)), dma((7, 2)), dma((2,)),
            dma((1,)), dma((UNITS,)), dma((1,)), dma((UNITS, 2)), dma((1,)), dma((UNITS, 2)),
            dma((1,)), dma((UNITS,)), dma((2,)),
            *[dma((2,))] * 7, dma((1,)), dma((7,)), dma((2,)), dma((4,)), dma((1,)), dma((7, 2)),
        ],
        compiler_params=pltpu.CompilerParams(
            collective_id=0, has_side_effects=True, vmem_limit_bytes=58 * 1024 * 1024
        ),
        cost_estimate=pl.CostEstimate(flops=5_900_000_000, bytes_accessed=12_000_000, transcendentals=512),
    )(
        residual_grad.reshape(8, 2, 16, 768), shortcut, hidden_in.reshape(16, 16, 768), key_value_gradient,
        key_value_weight, adapter_down_matrix.T, adapter_up,
    )
    return result, down.astype(f32).T, up.astype(f32)


def solution(mesh):
    part = P("dp", "tensor")
    return jax.shard_map(
        shards, mesh=mesh, in_specs=(part,) * 5 + (P(), P()),
        out_specs=(P(("dp", "tensor"), None), P(), P()), check_vma=False,
    )
```

```python
import jax
import jax.numpy as jnp
from jax import lax
from jax.experimental import pallas as pl
from jax.experimental.pallas import tpu as pltpu
from jax.sharding import PartitionSpec as P

MESH = pl.DeviceIdType.MESH
UNITS = 8
LAGS = (1, 2, 4, 5)
epsilon = 1e-05
adapter_scale = 0.25


def place(xh, z, y, xl, c):
    return {"dp": xh * 8 + z, "tensor": (y * 2 + xl) * 2 + c}


def contract(a, b):
    return lax.dot_general(a, b, (((1,), (1,)), ((), ())), preferred_element_type=jnp.float32)


def multiply(a, b):
    return jnp.dot(a, b, preferred_element_type=jnp.float32)


def contract_first(a, b):
    return lax.dot_general(a, b, (((0,), (0,)), ((), ())), preferred_element_type=jnp.float32)


def split(value):
    hi = value.astype(jnp.bfloat16)
    return hi, (value - hi.astype(jnp.float32)).astype(jnp.bfloat16)


def whole_kernel(
    grad_ref, short_ref, hidden_ref, kv_ref, kvw_ref, down_ref, up_ref,
    out_ref, down_out, up_out,
    blocks, weights, core_out, core_in, own, y_out, far_in, y_in, pair, x_out, x_in, fin_out, fin_in,
    hidden, hidden_in, kv_all, w_ring, down_rows, up_rows, sums_out, sums_in, sums_all, back_keep,
    norm_sum, norm_out, norm_in, g_out, g_in, g_all, g_rows,
    load_sem, a_send, a_recv, s_sem,
    core_send, core_recv, far_send, far_recv, near_send, near_recv, x_send, x_recv, f_sem,
    h_sem, k_sem, kc_sem, su_sem, sa_sem, n_sem, gs_sem, gd_sem, gt_send, gt_recv, gc_sem, t_sem, w_send, w_recv,
):
    p, q = lax.axis_index("dp"), lax.axis_index("tensor")
    xh, z = p // 8, p % 8
    y, xl, c = q // 4, (q // 2) % 2, q % 2

    def at(xh=xh, z=z, y=y, xl=xl, c=c):
        return place(xh, z, y, xl, c)

    up, down = at(z=(z + 1) % 8), at(z=(z + 7) % 8)
    core_peer = at(c=1 - c)
    xl_peer = at(xl=1 - xl)

    def local(source, target, i):
        return pltpu.make_async_copy(source, target, load_sem.at[i])

    loads = [local(grad_ref.at[:, h], blocks.at[7, h], h) for h in range(2)]
    loads.append(local(short_ref, weights.at[0], 2))
    loads.append(local(hidden_ref, hidden, 3))
    loads.append(local(hidden_ref.at[q], hidden_in.at[q], 4))
    loads.append(local(kv_ref, kv_all.at[q // 2, c], 5))
    loads.append(local(down_ref.at[:, pl.ds(pl.multiple_of(q * 768, 128), 768)], down_rows, 6))
    loads.append(local(up_ref, up_rows, 7))
    for l in loads:
        l.start()

    barrier = pltpu.get_barrier_semaphore()

    def each(body, count=16):
        def step(d, carry):
            body(d)
            return carry
        lax.fori_loop(1, count, step, 0)

    def turn(a, d):
        return lax.rem(a + d, 16)

    def greet(d):
        pl.semaphore_signal(barrier, inc=1, device_id={"dp": p, "tensor": turn(q, d)}, device_id_type=MESH)
        pl.semaphore_signal(barrier, inc=1, device_id={"dp": turn(p, d), "tensor": q}, device_id_type=MESH)

    each(greet)

    @pl.when(p != q)
    def _():
        pl.semaphore_signal(barrier, inc=1, device_id={"dp": q, "tensor": p}, device_id_type=MESH)

    for l in loads:
        l.wait()

    @pl.when(p != q)
    def _():
        pl.semaphore_wait(barrier, 31)

    @pl.when(p == q)
    def _():
        pl.semaphore_wait(barrier, 30)

    def remote(src, dst, send, recv, to):
        return pltpu.make_async_remote_copy(
            src_ref=src, dst_ref=dst, send_sem=send, recv_sem=recv, device_id=to, device_id_type=MESH
        )

    def group(ref, sems):
        return remote(ref, ref, sems.at[0], sems.at[1], core_peer)

    def ring_copy(buffer, send, recv, s, h):
        source = 7 if s < 2 else (4 + h if s == 6 else s - 2)
        way = (up, down)[h if s == 6 else s % 2]
        return remote(buffer.at[source, h], buffer.at[s, h], send.at[0], recv.at[s, h], way)

    def block_copy(s, h):
        return ring_copy(blocks, a_send, a_recv, s, h)

    def w_copy(s, h):
        return ring_copy(w_ring, w_send, w_recv, s, h)

    def ring_half(copy, t, h):
        if t == 3:
            copy(6, h).wait_recv()
            return
        for s in (2 * t, 2 * t + 1):
            copy(s, h).wait_recv()
            if s < 4:
                copy(s + 2, h).start()
            elif s - 4 == h:
                copy(6, h).start()

    def ring_step(copy, t):
        ring_half(copy, t, 0)
        ring_half(copy, t, 1)

    for h in range(2):
        for s in range(2):
            block_copy(s, h).start()

    def swap_copy():
        return remote(weights.at[0], weights.at[1], s_sem.at[0], s_sem.at[1], at(xh=1 - xh))

    swap_copy().start()

    def to_tensor(source, target, sems, d):
        return remote(source, target, sems.at[0], sems.at[1], {"dp": p, "tensor": turn(q, d)})

    def to_dp(source, target, sems, d):
        return remote(source, target, sems.at[0], sems.at[1], {"dp": turn(p, d), "tensor": q})

    def turn_copy(part):
        return remote(kvw_ref, w_ring.at[7, part], t_sem.at[0], t_sem.at[1], {"dp": q, "tensor": p})

    def turn_local():
        return pltpu.make_async_copy(kvw_ref, w_ring.at[7, xh], t_sem.at[0])

    def half_copy(part):
        return remote(w_ring.at[7, part], w_ring.at[7, part], t_sem.at[2], t_sem.at[3], at(xh=1 - xh))

    @pl.when(p != q)
    def _():
        turn_copy(q // 8).start()

    @pl.when(p == q)
    def _():
        turn_local().start()

    down_hi, down_lo = split(down_rows[...])
    mine = hidden[...].reshape(256, 768)
    low = contract(mine, jnp.concatenate([down_hi, down_lo], axis=0))
    wide = mine.astype(jnp.float32)
    squares = jnp.sum(wide * wide, axis=1, keepdims=True)
    sums = jnp.concatenate([low[:, :64] + low[:, 64:], jnp.broadcast_to(squares, (256, 64))], axis=1)
    sums_out[...] = sums.reshape(16, 16, 128)
    each(lambda d: to_tensor(sums_out.at[turn(q, d)], sums_in.at[q], su_sem, d).start())
    sums_in[q] = sums_out[q]

    def kv_send():
        each(lambda e: to_tensor(kv_ref, kv_all.at[q // 2, c], k_sem, 2 * e).start(), 8)

    def kv_core_copy():
        return remote(kv_all.at[:, c], kv_all.at[:, c], kc_sem.at[0], kc_sem.at[1], core_peer)

    def kv_forward():
        group(kv_all.at[pl.ds(0, 7), 0], k_sem).wait_recv()
        kv_core_copy().start()

    def hidden_send():
        each(lambda d: to_tensor(hidden_ref.at[turn(q, d)], hidden_in.at[q], h_sem, d).start())

    def sums_reduce():
        group(sums_in.at[pl.ds(0, 15)], su_sem).wait_recv()
        sums_all[q] = jnp.sum(sums_in[...], axis=0)
        each(lambda d: to_tensor(sums_all.at[q], sums_all.at[q], sa_sem, d).start())

    def adapter_parts():
        group(sums_all.at[pl.ds(0, 15)], sa_sem).wait_recv()
        kv_core_copy().wait_recv()
        both = jnp.zeros((256, 128), jnp.float32)
        for s in range(16):
            hi, lo = split(up_rows[:, 128 * s : 128 * s + 128])
            both = both + contract(kv_all[s // 2, s % 2], jnp.concatenate([hi, lo], axis=0))
        back = both[:, :64] + both[:, 64:]
        back_keep[...] = back
        reduced = sums_all[...].reshape(256, 128)
        scale = lax.rsqrt(reduced[:, 64:65] / 12288 + epsilon)
        low = jnp.concatenate(split(scale * reduced[:, :64]), axis=1)
        upper = contract_first(low, kv_all[q // 2, c])
        g_out[8:16, 24:32] = jnp.zeros((8, 8, 128), jnp.float32)
        g_out[0:8, 24:32] = (adapter_scale * (upper[:64] + upper[64:])).reshape(8, 8, 128)
        scaled = jnp.concatenate(split(scale * back), axis=1)
        lower = contract_first(scaled, hidden[...].reshape(256, 768))
        lower = adapter_scale * (lower[:64] + lower[64:])
        for b in range(6):
            g_rows[64 * b : 64 * b + 64] = lower[:, 128 * b : 128 * b + 128]
        g_out[:, 0:24] = g_rows[...].reshape(16, 24, 128)
        each(lambda d: to_dp(g_out.at[turn(p, d)], g_in.at[p], gs_sem, d).start())
        g_in[p] = g_out[p]

    def grads_reduce():
        group(g_in.at[pl.ds(0, 15)], gs_sem).wait_recv()
        g_all[q, p] = jnp.sum(g_in[...], axis=0).astype(jnp.bfloat16)
        each(lambda d: to_dp(g_all.at[q, p], g_all.at[q, p], gd_sem, d).start())

    def chips_copy(s, e):
        return remote(
            g_all.at[s], g_all.at[s], gt_send.at[0], gt_recv.at[e - 1], {"dp": p, "tensor": turn(q, 2 * e)}
        )

    def other_core_copy(s):
        return remote(g_all.at[s], g_all.at[s], gc_sem.at[0], gc_sem.at[1], core_peer)

    def grads_spread():
        group(g_all.at[q, pl.ds(0, 15)], gd_sem).wait_recv()
        each(lambda e: chips_copy(q, e).start(), 8)
        other_core_copy(q).start()

    def grads_forward():
        def body(e):
            s = turn(q, 16 - 2 * e)
            chips_copy(s, e).wait_recv()
            other_core_copy(s).start()
        each(body, 8)

    def block_z(s):
        half = (s + 2) // 2
        return lax.rem(z + 8 + jnp.where(s == 7, 0, jnp.where(s % 2 == 0, -half, half)), 8)

    def norm_term(slots):
        left = [kv_all[4 * part + block_z(s) // 2, block_z(s) % 2] for s in slots for part in range(2)]
        right = [w_ring[s, part] for s in slots for part in range(2)]
        return contract(jnp.concatenate(left, axis=1), jnp.concatenate(right, axis=1))

    def norm_begin():
        half_copy(1 - xh).wait_recv()
        for h in range(2):
            for s in range(2):
                w_copy(s, h).start()

    def norm_half(t):
        ring_half(w_copy, t, 0)

    def norm_hop(t):
        ring_half(w_copy, t, 1)
        term = norm_term((2 * t, 2 * t + 1))
        norm_sum[...] = term if t == 0 else norm_sum[...] + term

    def norm_send():
        back_hi, back_lo = split(back_keep[...])
        down_hi, down_lo = split(down_rows[...])
        extra = multiply(
            jnp.concatenate([back_hi, back_lo], axis=1), jnp.concatenate([down_hi, down_hi], axis=0)
        ) + multiply(back_hi, down_lo)
        total = norm_sum[...] + adapter_scale * extra
        norm_out[...] = total.astype(jnp.bfloat16).reshape(16, 16, 768)
        each(lambda d: to_tensor(norm_out.at[turn(q, d)], norm_in.at[q], n_sem, d).start())
        norm_in[q] = norm_out[q]

    def turn_done():
        @pl.when(p != q)
        def _():
            turn_copy(xh).wait_recv()

        @pl.when(p == q)
        def _():
            turn_local().wait()

        half_copy(xh).start()

    def core_copy(i):
        return remote(core_out.at[i], core_in.at[i], core_send.at[0], core_recv.at[i], core_peer)

    def far_copy(i, way):
        return remote(
            y_out.at[i, (y + 2) % 4, way], far_in.at[i, way], far_send.at[0], far_recv.at[i, way],
            at(y=(y + 1 + 2 * way) % 4),
        )

    def near_copy(i, way):
        to = (y + 1 + 2 * way) % 4
        return remote(y_out.at[i, to], y_in.at[i, way], near_send.at[0], near_recv.at[i, way], at(y=to))

    def x_copy(i):
        return remote(x_out.at[i], x_in.at[i], x_send.at[0], x_recv.at[i], xl_peer)

    def side_of(i):
        return jnp.where(i > 4, 1, jnp.where(i == 3, 1, 0))

    def pair_of(i):
        return jnp.where(i > 4, i - 4, jnp.where(i == 4, 3, jnp.where(i == 3, 0, i)))

    def fin_slot(i):
        g = side_of(i)
        return (xh + g - 2 * xh * g) * 8 + z

    before = {
        0: [lambda: ring_step(block_copy, 0)],
        1: [lambda: ring_step(block_copy, 1)],
        2: [lambda: ring_step(block_copy, 2)],
        3: [lambda: swap_copy().wait_recv()],
        4: [lambda: ring_step(block_copy, 3)],
    }
    after = {
        0: [turn_done, kv_send],
        1: [sums_reduce],
        2: [norm_begin, kv_forward],
        3: [hidden_send],
        4: [adapter_parts, lambda: norm_half(0)],
        5: [lambda: norm_hop(0)],
        6: [grads_reduce, lambda: norm_half(1)],
        7: [lambda: norm_hop(1)],
        8: [grads_spread, lambda: norm_half(2)],
        9: [lambda: norm_hop(2)],
        10: [lambda: norm_half(3), grads_forward],
        11: [lambda: norm_hop(3), norm_send],
    }

    def run(table, i):
        for when, acts in table.items():
            @pl.when(i == when)
            def _(acts=acts):
                for act in acts:
                    act()

    def step(i, carry):
        run(before, i)

        @pl.when(i < UNITS)
        def _():
            t, g = pair_of(i), side_of(i)
            both = contract(blocks[pl.ds(2 * t, 2)].reshape(512, 768), weights[g]).reshape(2, 2, 4, 32, 768)
            first, second = both[:, 0], both[:, 1]
            theirs = jnp.where(c == 0, second, first).astype(jnp.bfloat16)
            mine = jnp.where(c == 0, first, second)
            for b in range(2):
                core_out[i, :, b] = theirs[b]
            core_copy(i).start()
            for b in range(2):
                own[i, :, b] = mine[b]

        j = i - LAGS[0]

        @pl.when(jnp.logical_and(j >= 0, j < UNITS))
        def _():
            core_copy(j).wait_recv()
            total = own[j] + core_in[j].astype(jnp.float32)
            own[j] = total
            y_out[j] = total.astype(jnp.bfloat16)
            far_copy(j, 0).start()
            far_copy(j, 1).start()

        r = i - LAGS[1]

        @pl.when(jnp.logical_and(r >= 0, r < UNITS))
        def _():
            for way in range(2):
                far_copy(r, way).wait_recv()
                to = (y + 1 + 2 * way) % 4
                y_out[r, to, way] = (own[r, to, way] + far_in[r, way].astype(jnp.float32)).astype(jnp.bfloat16)
                near_copy(r, way).start()

        m = i - LAGS[2]

        @pl.when(jnp.logical_and(m >= 0, m < UNITS))
        def _():
            for way in range(2):
                near_copy(m, way).wait_recv()
            got = y_in[m].astype(jnp.float32)
            total = (own[m, y] + (got[0] + got[1])).reshape(2, 2, 16, 768)
            pair[m] = total
            for b in range(2):
                x_out[m, b] = pair[m, b, 1 - xl].astype(jnp.bfloat16)
            x_copy(m).start()

        n = i - LAGS[3]

        @pl.when(jnp.logical_and(n >= 0, n < UNITS))
        def _():
            x_copy(n).wait_recv()
            for b in range(2):
                done = (pair[n, b, xl] + x_in[n, b].astype(jnp.float32)).astype(jnp.bfloat16)
                s = 2 * pair_of(n) + b
                slot = fin_slot(n)

                @pl.when(s == 7)
                def _():
                    fin_in[slot] = done

                @pl.when(s != 7)
                def _():
                    fin_out[n, b] = done
                    remote(
                        fin_out.at[n, b], fin_in.at[slot], f_sem.at[0], f_sem.at[1], at(z=block_z(s))
                    ).start()

        run(after, i)
        return carry

    lax.fori_loop(0, UNITS + LAGS[3], step, 0)

    group(g_all.at[pl.ds(0, 8)], gc_sem).wait_recv()

    def unpack(s, carry):
        packed = g_all[s].astype(jnp.float32)
        lower = packed[:, :24].reshape(6, 64, 128)
        for b in range(6):
            down_out[:, pl.ds(pl.multiple_of(s * 768 + 128 * b, 128), 128)] = lower[b].astype(down_out.dtype)
        up_out[:, pl.ds(pl.multiple_of(s * 128, 128), 128)] = packed[:8, 24:].reshape(64, 128).astype(up_out.dtype)
        return carry

    lax.fori_loop(0, 16, unpack, 0)

    group(hidden_in.at[pl.ds(0, 15)], h_sem).wait_recv()
    group(norm_in.at[pl.ds(0, 15)], n_sem).wait_recv()
    my_scale = lax.rsqrt(sums_all[q][:, 64:65] / 12288 + epsilon)

    def dots(s, total):
        return total + hidden_in[s].astype(jnp.float32) * norm_in[s].astype(jnp.float32)

    products = lax.fori_loop(0, 16, dots, jnp.zeros((16, 768), jnp.float32))
    inner = jnp.sum(products, axis=1, keepdims=True) * my_scale / 12288
    group(fin_in.at[pl.ds(0, 14)], f_sem).wait_recv()

    def take(s, carry):
        normed = hidden_in[s].astype(jnp.float32) * my_scale
        done = fin_in[s].astype(jnp.float32) + my_scale * (norm_in[s].astype(jnp.float32) - normed * inner)
        out_ref[:, pl.ds(pl.multiple_of(s * 768, 128), 768)] = done.astype(out_ref.dtype)
        return carry

    lax.fori_loop(0, 16, take, 0)

    def gone(ref, sems):
        remote(ref, ref, sems.at[0], sems.at[0], core_peer).wait_send()

    gone(blocks.at[pl.ds(0, 7)], a_send)
    gone(w_ring.at[pl.ds(0, 7)], w_send)
    swap_copy().wait_send()
    gone(core_out, core_send)
    gone(far_in, far_send)
    gone(y_in, near_send)
    gone(x_out, x_send)
    gone(fin_in.at[pl.ds(0, 14)], f_sem)
    half_copy(xh).wait_send()

    @pl.when(p != q)
    def _():
        turn_copy(q // 8).wait_send()

    gone(sums_in.at[pl.ds(0, 15)], su_sem)
    gone(sums_all.at[pl.ds(0, 15)], sa_sem)
    gone(kv_all.at[pl.ds(0, 7), 0], k_sem)
    kv_core_copy().wait_send()
    gone(hidden_in.at[pl.ds(0, 15)], h_sem)
    gone(norm_in.at[pl.ds(0, 15)], n_sem)
    gone(g_in.at[pl.ds(0, 15)], gs_sem)
    gone(g_all.at[0, pl.ds(0, 15)], gd_sem)
    gone(g_all.at[pl.ds(0, 7)], gt_send)
    gone(g_all.at[pl.ds(0, 8)], gc_sem)


def shards(hidden_in, residual_grad, key_value_gradient, shortcut, key_value_weight, adapter_down_matrix, adapter_up):
    bf, f32, dma = jnp.bfloat16, jnp.float32, pltpu.SemaphoreType.DMA
    v = pltpu.VMEM
    result, down, up = pl.pallas_call(
        whole_kernel,
        out_shape=[
            jax.ShapeDtypeStruct((16, 12288), bf),
            jax.ShapeDtypeStruct((64, 12288), bf),
            jax.ShapeDtypeStruct((64, 2048), bf),
        ],
        in_specs=[pl.BlockSpec(memory_space=pl.ANY)] * 7,
        out_specs=[pl.BlockSpec(memory_space=pltpu.VMEM)] * 3,
        scratch_shapes=[
            v((8, 2, 8, 16, 768), bf), v((2, 768, 768), bf),
            v((UNITS, 4, 2, 32, 768), bf), v((UNITS, 4, 2, 32, 768), bf), v((UNITS, 4, 2, 32, 768), f32),
            v((UNITS, 4, 2, 32, 768), bf), v((UNITS, 2, 32, 768), bf), v((UNITS, 2, 2, 32, 768), bf),
            v((UNITS, 2, 2, 16, 768), f32), v((UNITS, 2, 16, 768), bf), v((UNITS, 2, 16, 768), bf),
            v((UNITS, 2, 16, 768), bf), v((16, 16, 768), bf),
            v((16, 16, 768), bf), v((16, 16, 768), bf), v((8, 2, 256, 128), bf), v((8, 2, 768, 128), bf),
            v((64, 768), f32), v((64, 2048), f32), v((16, 16, 128), f32), v((16, 16, 128), f32),
            v((16, 16, 128), f32), v((256, 64), f32),
            v((256, 768), f32), v((16, 16, 768), bf), v((16, 16, 768), bf),
            v((16, 32, 128), f32), v((16, 32, 128), f32), v((16, 16, 32, 128), bf), v((384, 128), f32),
            dma((8,)), dma((1,)), dma((7, 2)), dma((2,)),
            dma((1,)), dma((UNITS,)), dma((1,)), dma((UNITS, 2)), dma((1,)), dma((UNITS, 2)),
            dma((1,)), dma((UNITS,)), dma((2,)),
            *[dma((2,))] * 8, dma((1,)), dma((7,)), dma((2,)), dma((4,)), dma((1,)), dma((7, 2)),
        ],
        compiler_params=pltpu.CompilerParams(
            collective_id=0, has_side_effects=True, vmem_limit_bytes=58 * 1024 * 1024
        ),
        cost_estimate=pl.CostEstimate(flops=5_900_000_000, bytes_accessed=12_000_000, transcendentals=512),
    )(
        residual_grad.reshape(8, 2, 16, 768), shortcut, hidden_in.reshape(16, 16, 768), key_value_gradient,
        key_value_weight, adapter_down_matrix.T, adapter_up,
    )
    return result, down.astype(f32).T, up.astype(f32)


def solution(mesh):
    part = P("dp", "tensor")
    return jax.shard_map(
        shards, mesh=mesh, in_specs=(part,) * 5 + (P(), P()),
        out_specs=(P(("dp", "tensor"), None), P(), P()), check_vma=False,
    )
```

```python
import jax
import jax.numpy as jnp
from jax import lax
from jax.experimental import pallas as pl
from jax.experimental.pallas import tpu as pltpu
from jax.sharding import PartitionSpec as P

MESH = pl.DeviceIdType.MESH
UNITS = 8
LAGS = (1, 2, 4, 6)
epsilon = 1e-05
adapter_scale = 0.25


def place(xh, z, y, xl, c):
    return {"dp": xh * 8 + z, "tensor": (y * 2 + xl) * 2 + c}


def contract(a, b):
    return lax.dot_general(a, b, (((1,), (1,)), ((), ())), preferred_element_type=jnp.float32)


def multiply(a, b):
    return jnp.dot(a, b, preferred_element_type=jnp.float32)


def contract_first(a, b):
    return lax.dot_general(a, b, (((0,), (0,)), ((), ())), preferred_element_type=jnp.float32)


def split(value):
    hi = value.astype(jnp.bfloat16)
    return hi, (value - hi.astype(jnp.float32)).astype(jnp.bfloat16)


def whole_kernel(
    grad_ref, short_ref, hidden_ref, kv_ref, kvw_ref, down_ref, up_ref,
    out_ref, down_out, up_out,
    blocks, weights, core_out, core_in, own, y_out, far_in, y_in, pair, x_out, x_in, fin_out, fin_in,
    hidden, hidden_in, kv_all, w_ring, down_rows, up_rows, sums_out, sums_in, sums_all, back_keep,
    norm_sum, norm_out, norm_in, g_out, g_wire, g_in, g_all, g_rows,
    load_sem, a_send, a_recv, s_sem,
    core_send, core_recv, far_send, far_recv, near_send, near_recv, x_send, x_recv, f_sem,
    h_sem, k_sem, kc_sem, su_sem, sa_sem, n_sem, gs_sem, gd_sem, gt_send, gt_recv, gc_sem, t_sem, w_send, w_recv,
):
    p, q = lax.axis_index("dp"), lax.axis_index("tensor")
    xh, z = p // 8, p % 8
    y, xl, c = q // 4, (q // 2) % 2, q % 2

    def at(xh=xh, z=z, y=y, xl=xl, c=c):
        return place(xh, z, y, xl, c)

    up, down = at(z=(z + 1) % 8), at(z=(z + 7) % 8)
    core_peer = at(c=1 - c)
    xl_peer = at(xl=1 - xl)

    def local(source, target, i):
        return pltpu.make_async_copy(source, target, load_sem.at[i])

    loads = [local(grad_ref.at[:, h], blocks.at[7, h], h) for h in range(2)]
    loads.append(local(short_ref, weights.at[0], 2))
    loads.append(local(hidden_ref, hidden, 3))
    loads.append(local(hidden_ref.at[q], hidden_in.at[q], 4))
    loads.append(local(kv_ref, kv_all.at[q // 2, c], 5))
    loads.append(local(down_ref.at[:, pl.ds(pl.multiple_of(q * 768, 128), 768)], down_rows, 6))
    loads.append(local(up_ref, up_rows, 7))
    for l in loads:
        l.start()

    barrier = pltpu.get_barrier_semaphore()

    def each(body, count=16):
        def step(d, carry):
            body(d)
            return carry
        lax.fori_loop(1, count, step, 0)

    def turn(a, d):
        return lax.rem(a + d, 16)

    def greet(d):
        pl.semaphore_signal(barrier, inc=1, device_id={"dp": p, "tensor": turn(q, d)}, device_id_type=MESH)
        pl.semaphore_signal(barrier, inc=1, device_id={"dp": turn(p, d), "tensor": q}, device_id_type=MESH)

    each(greet)

    @pl.when(p != q)
    def _():
        pl.semaphore_signal(barrier, inc=1, device_id={"dp": q, "tensor": p}, device_id_type=MESH)

    for l in loads:
        l.wait()

    @pl.when(p != q)
    def _():
        pl.semaphore_wait(barrier, 31)

    @pl.when(p == q)
    def _():
        pl.semaphore_wait(barrier, 30)

    def remote(src, dst, send, recv, to):
        return pltpu.make_async_remote_copy(
            src_ref=src, dst_ref=dst, send_sem=send, recv_sem=recv, device_id=to, device_id_type=MESH
        )

    def group(ref, sems):
        return remote(ref, ref, sems.at[0], sems.at[1], core_peer)

    def ring_copy(buffer, send, recv, s, h):
        source = 7 if s < 2 else (4 + h if s == 6 else s - 2)
        way = (up, down)[h if s == 6 else s % 2]
        return remote(buffer.at[source, h], buffer.at[s, h], send.at[0], recv.at[s, h], way)

    def block_copy(s, h):
        return ring_copy(blocks, a_send, a_recv, s, h)

    def w_copy(s, h):
        return ring_copy(w_ring, w_send, w_recv, s, h)

    def ring_half(copy, t, h):
        if t == 3:
            copy(6, h).wait_recv()
            return
        for s in (2 * t, 2 * t + 1):
            copy(s, h).wait_recv()
            if s < 4:
                copy(s + 2, h).start()
            elif s - 4 == h:
                copy(6, h).start()

    def ring_step(copy, t):
        ring_half(copy, t, 0)
        ring_half(copy, t, 1)

    for h in range(2):
        for s in range(2):
            block_copy(s, h).start()

    def swap_copy():
        return remote(weights.at[0], weights.at[1], s_sem.at[0], s_sem.at[1], at(xh=1 - xh))

    swap_copy().start()

    def to_tensor(source, target, sems, d):
        return remote(source, target, sems.at[0], sems.at[1], {"dp": p, "tensor": turn(q, d)})

    def to_dp(source, target, sems, d):
        return remote(source, target, sems.at[0], sems.at[1], {"dp": turn(p, d), "tensor": q})

    def turn_copy(part):
        return remote(kvw_ref, w_ring.at[7, part], t_sem.at[0], t_sem.at[1], {"dp": q, "tensor": p})

    def turn_local():
        return pltpu.make_async_copy(kvw_ref, w_ring.at[7, xh], t_sem.at[0])

    def half_copy(part):
        return remote(w_ring.at[7, part], w_ring.at[7, part], t_sem.at[2], t_sem.at[3], at(xh=1 - xh))

    @pl.when(p != q)
    def _():
        turn_copy(q // 8).start()

    @pl.when(p == q)
    def _():
        turn_local().start()

    down_hi, down_lo = split(down_rows[...])
    mine = hidden[...].reshape(256, 768)
    low = contract(mine, jnp.concatenate([down_hi, down_lo], axis=0))
    wide = mine.astype(jnp.float32)
    squares = jnp.sum(wide * wide, axis=1, keepdims=True)
    sums = jnp.concatenate([low[:, :64] + low[:, 64:], jnp.broadcast_to(squares, (256, 64))], axis=1)
    sums_out[...] = sums.reshape(16, 16, 128)
    each(lambda d: to_tensor(sums_out.at[turn(q, d)], sums_in.at[q], su_sem, d).start())
    sums_in[q] = sums_out[q]

    def kv_send():
        each(lambda e: to_tensor(kv_ref, kv_all.at[q // 2, c], k_sem, 2 * e).start(), 8)

    def kv_core_copy():
        return remote(kv_all.at[:, c], kv_all.at[:, c], kc_sem.at[0], kc_sem.at[1], core_peer)

    def kv_forward():
        group(kv_all.at[pl.ds(0, 7), 0], k_sem).wait_recv()
        kv_core_copy().start()

    def hidden_send():
        each(lambda d: to_tensor(hidden_ref.at[turn(q, d)], hidden_in.at[q], h_sem, d).start())

    def sums_reduce():
        group(sums_in.at[pl.ds(0, 15)], su_sem).wait_recv()
        sums_all[q] = jnp.sum(sums_in[...], axis=0)
        each(lambda d: to_tensor(sums_all.at[q], sums_all.at[q], sa_sem, d).start())

    def adapter_parts():
        group(sums_all.at[pl.ds(0, 15)], sa_sem).wait_recv()
        kv_core_copy().wait_recv()
        both = jnp.zeros((256, 128), jnp.float32)
        for s in range(16):
            hi, lo = split(up_rows[:, 128 * s : 128 * s + 128])
            both = both + contract(kv_all[s // 2, s % 2], jnp.concatenate([hi, lo], axis=0))
        back = both[:, :64] + both[:, 64:]
        back_keep[...] = back
        reduced = sums_all[...].reshape(256, 128)
        scale = lax.rsqrt(reduced[:, 64:65] / 12288 + epsilon)
        low = jnp.concatenate(split(scale * reduced[:, :64]), axis=1)
        upper = contract_first(low, kv_all[q // 2, c])
        g_out[8:16, 24:32] = jnp.zeros((8, 8, 128), jnp.float32)
        g_out[0:8, 24:32] = (adapter_scale * (upper[:64] + upper[64:])).reshape(8, 8, 128)
        scaled = jnp.concatenate(split(scale * back), axis=1)
        lower = contract_first(scaled, hidden[...].reshape(256, 768))
        lower = adapter_scale * (lower[:64] + lower[64:])
        for b in range(6):
            g_rows[64 * b : 64 * b + 64] = lower[:, 128 * b : 128 * b + 128]
        g_out[:, 0:24] = g_rows[...].reshape(16, 24, 128)
        g_wire[...] = g_out[...].astype(jnp.bfloat16)
        each(lambda d: to_dp(g_wire.at[turn(p, d)], g_in.at[p], gs_sem, d).start())
        g_in[p] = g_wire[p]

    def grads_reduce():
        group(g_in.at[pl.ds(0, 15)], gs_sem).wait_recv()
        g_all[q, p] = jnp.sum(g_in[...].astype(jnp.float32), axis=0).astype(jnp.bfloat16)
        each(lambda d: to_dp(g_all.at[q, p], g_all.at[q, p], gd_sem, d).start())

    def chips_copy(s, e):
        return remote(
            g_all.at[s], g_all.at[s], gt_send.at[0], gt_recv.at[e - 1], {"dp": p, "tensor": turn(q, 2 * e)}
        )

    def other_core_copy(s):
        return remote(g_all.at[s], g_all.at[s], gc_sem.at[0], gc_sem.at[1], core_peer)

    def grads_spread():
        group(g_all.at[q, pl.ds(0, 15)], gd_sem).wait_recv()
        each(lambda e: chips_copy(q, e).start(), 8)
        other_core_copy(q).start()

    def grads_forward():
        def body(e):
            s = turn(q, 16 - 2 * e)
            chips_copy(s, e).wait_recv()
            other_core_copy(s).start()
        each(body, 8)

    def block_z(s):
        half = (s + 2) // 2
        return lax.rem(z + 8 + jnp.where(s == 7, 0, jnp.where(s % 2 == 0, -half, half)), 8)

    def norm_term(slots):
        left = [kv_all[4 * part + block_z(s) // 2, block_z(s) % 2] for s in slots for part in range(2)]
        right = [w_ring[s, part] for s in slots for part in range(2)]
        return contract(jnp.concatenate(left, axis=1), jnp.concatenate(right, axis=1))

    def norm_begin():
        half_copy(1 - xh).wait_recv()
        for h in range(2):
            for s in range(2):
                w_copy(s, h).start()

    def norm_half(t):
        ring_half(w_copy, t, 0)

    def norm_hop(t):
        ring_half(w_copy, t, 1)
        term = norm_term((2 * t, 2 * t + 1))
        norm_sum[...] = term if t == 0 else norm_sum[...] + term

    def norm_send():
        back_hi, back_lo = split(back_keep[...])
        down_hi, down_lo = split(down_rows[...])
        extra = multiply(
            jnp.concatenate([back_hi, back_lo], axis=1), jnp.concatenate([down_hi, down_hi], axis=0)
        ) + multiply(back_hi, down_lo)
        total = norm_sum[...] + adapter_scale * extra
        norm_out[...] = total.astype(jnp.bfloat16).reshape(16, 16, 768)
        each(lambda d: to_tensor(norm_out.at[turn(q, d)], norm_in.at[q], n_sem, d).start())
        norm_in[q] = norm_out[q]

    def turn_done():
        @pl.when(p != q)
        def _():
            turn_copy(xh).wait_recv()

        @pl.when(p == q)
        def _():
            turn_local().wait()

        half_copy(xh).start()

    def core_copy(i):
        return remote(core_out.at[i], core_in.at[i], core_send.at[0], core_recv.at[i], core_peer)

    def far_copy(i, way):
        return remote(
            y_out.at[i, (y + 2) % 4, way], far_in.at[i, way], far_send.at[0], far_recv.at[i, way],
            at(y=(y + 1 + 2 * way) % 4),
        )

    def near_copy(i, way):
        to = (y + 1 + 2 * way) % 4
        return remote(y_out.at[i, to], y_in.at[i, way], near_send.at[0], near_recv.at[i, way], at(y=to))

    def x_copy(i):
        return remote(x_out.at[i], x_in.at[i], x_send.at[0], x_recv.at[i], xl_peer)

    def side_of(i):
        return jnp.where(i > 4, 1, jnp.where(i == 3, 1, 0))

    def pair_of(i):
        return jnp.where(i > 4, i - 4, jnp.where(i == 4, 3, jnp.where(i == 3, 0, i)))

    def fin_slot(i):
        g = side_of(i)
        return (xh + g - 2 * xh * g) * 8 + z

    before = {
        0: [lambda: ring_step(block_copy, 0)],
        1: [lambda: ring_step(block_copy, 1)],
        2: [lambda: ring_step(block_copy, 2)],
        3: [lambda: swap_copy().wait_recv()],
        4: [lambda: ring_step(block_copy, 3)],
    }
    after = {
        0: [turn_done, kv_send],
        1: [sums_reduce, hidden_send],
        2: [norm_begin, kv_forward],
        4: [adapter_parts, lambda: norm_half(0)],
        5: [lambda: norm_hop(0)],
        6: [grads_reduce, lambda: norm_half(1)],
        7: [lambda: norm_hop(1)],
        8: [grads_spread, lambda: norm_half(2)],
        9: [lambda: norm_hop(2)],
        10: [lambda: norm_half(3), grads_forward],
        11: [lambda: norm_hop(3), norm_send],
    }

    def run(table, i):
        for when, acts in table.items():
            @pl.when(i == when)
            def _(acts=acts):
                for act in acts:
                    act()

    def step(i, carry):
        run(before, i)

        @pl.when(i < UNITS)
        def _():
            t, g = pair_of(i), side_of(i)
            both = contract(blocks[pl.ds(2 * t, 2)].reshape(512, 768), weights[g]).reshape(2, 2, 4, 32, 768)
            first, second = both[:, 0], both[:, 1]
            theirs = jnp.where(c == 0, second, first).astype(jnp.bfloat16)
            mine = jnp.where(c == 0, first, second)
            for b in range(2):
                core_out[i, :, b] = theirs[b]
            core_copy(i).start()
            for b in range(2):
                own[i, :, b] = mine[b]

        j = i - LAGS[0]

        @pl.when(jnp.logical_and(j >= 0, j < UNITS))
        def _():
            core_copy(j).wait_recv()
            total = own[j] + core_in[j].astype(jnp.float32)
            own[j] = total
            y_out[j] = total.astype(jnp.bfloat16)
            far_copy(j, 0).start()
            far_copy(j, 1).start()

        r = i - LAGS[1]

        @pl.when(jnp.logical_and(r >= 0, r < UNITS))
        def _():
            for way in range(2):
                far_copy(r, way).wait_recv()
                to = (y + 1 + 2 * way) % 4
                y_out[r, to, way] = (own[r, to, way] + far_in[r, way].astype(jnp.float32)).astype(jnp.bfloat16)
                near_copy(r, way).start()

        m = i - LAGS[2]

        @pl.when(jnp.logical_and(m >= 0, m < UNITS))
        def _():
            for way in range(2):
                near_copy(m, way).wait_recv()
            got = y_in[m].astype(jnp.float32)
            total = (own[m, y] + (got[0] + got[1])).reshape(2, 2, 16, 768)
            pair[m] = total
            for b in range(2):
                x_out[m, b] = pair[m, b, 1 - xl].astype(jnp.bfloat16)
            x_copy(m).start()

        n = i - LAGS[3]

        @pl.when(jnp.logical_and(n >= 0, n < UNITS))
        def _():
            x_copy(n).wait_recv()
            for b in range(2):
                done = (pair[n, b, xl] + x_in[n, b].astype(jnp.float32)).astype(jnp.bfloat16)
                s = 2 * pair_of(n) + b
                slot = fin_slot(n)

                @pl.when(s == 7)
                def _():
                    fin_in[slot] = done

                @pl.when(s != 7)
                def _():
                    fin_out[n, b] = done
                    remote(
                        fin_out.at[n, b], fin_in.at[slot], f_sem.at[0], f_sem.at[1], at(z=block_z(s))
                    ).start()

        run(after, i)
        return carry

    lax.fori_loop(0, UNITS + LAGS[3], step, 0)

    group(g_all.at[pl.ds(0, 8)], gc_sem).wait_recv()

    def unpack(s, carry):
        packed = g_all[s].astype(jnp.float32)
        lower = packed[:, :24].reshape(6, 64, 128)
        for b in range(6):
            down_out[:, pl.ds(pl.multiple_of(s * 768 + 128 * b, 128), 128)] = lower[b].astype(down_out.dtype)
        up_out[:, pl.ds(pl.multiple_of(s * 128, 128), 128)] = packed[:8, 24:].reshape(64, 128).astype(up_out.dtype)
        return carry

    lax.fori_loop(0, 16, unpack, 0)

    group(hidden_in.at[pl.ds(0, 15)], h_sem).wait_recv()
    group(norm_in.at[pl.ds(0, 15)], n_sem).wait_recv()
    my_scale = lax.rsqrt(sums_all[q][:, 64:65] / 12288 + epsilon)

    def dots(s, total):
        return total + hidden_in[s].astype(jnp.float32) * norm_in[s].astype(jnp.float32)

    products = lax.fori_loop(0, 16, dots, jnp.zeros((16, 768), jnp.float32))
    inner = jnp.sum(products, axis=1, keepdims=True) * my_scale / 12288
    group(fin_in.at[pl.ds(0, 14)], f_sem).wait_recv()

    def take(s, carry):
        normed = hidden_in[s].astype(jnp.float32) * my_scale
        done = fin_in[s].astype(jnp.float32) + my_scale * (norm_in[s].astype(jnp.float32) - normed * inner)
        out_ref[:, pl.ds(pl.multiple_of(s * 768, 128), 768)] = done.astype(out_ref.dtype)
        return carry

    lax.fori_loop(0, 16, take, 0)

    def gone(ref, sems):
        remote(ref, ref, sems.at[0], sems.at[0], core_peer).wait_send()

    gone(blocks.at[pl.ds(0, 7)], a_send)
    gone(w_ring.at[pl.ds(0, 7)], w_send)
    swap_copy().wait_send()
    gone(core_out, core_send)
    gone(far_in, far_send)
    gone(y_in, near_send)
    gone(x_out, x_send)
    gone(fin_in.at[pl.ds(0, 14)], f_sem)
    half_copy(xh).wait_send()

    @pl.when(p != q)
    def _():
        turn_copy(q // 8).wait_send()

    gone(sums_in.at[pl.ds(0, 15)], su_sem)
    gone(sums_all.at[pl.ds(0, 15)], sa_sem)
    gone(kv_all.at[pl.ds(0, 7), 0], k_sem)
    kv_core_copy().wait_send()
    gone(hidden_in.at[pl.ds(0, 15)], h_sem)
    gone(norm_in.at[pl.ds(0, 15)], n_sem)
    gone(g_in.at[pl.ds(0, 15)], gs_sem)
    gone(g_all.at[0, pl.ds(0, 15)], gd_sem)
    gone(g_all.at[pl.ds(0, 7)], gt_send)
    gone(g_all.at[pl.ds(0, 8)], gc_sem)


def shards(hidden_in, residual_grad, key_value_gradient, shortcut, key_value_weight, adapter_down_matrix, adapter_up):
    bf, f32, dma = jnp.bfloat16, jnp.float32, pltpu.SemaphoreType.DMA
    v = pltpu.VMEM
    result, down, up = pl.pallas_call(
        whole_kernel,
        out_shape=[
            jax.ShapeDtypeStruct((16, 12288), bf),
            jax.ShapeDtypeStruct((64, 12288), bf),
            jax.ShapeDtypeStruct((64, 2048), bf),
        ],
        in_specs=[pl.BlockSpec(memory_space=pl.ANY)] * 7,
        out_specs=[pl.BlockSpec(memory_space=pltpu.VMEM)] * 3,
        scratch_shapes=[
            v((8, 2, 8, 16, 768), bf), v((2, 768, 768), bf),
            v((UNITS, 4, 2, 32, 768), bf), v((UNITS, 4, 2, 32, 768), bf), v((UNITS, 4, 2, 32, 768), f32),
            v((UNITS, 4, 2, 32, 768), bf), v((UNITS, 2, 32, 768), bf), v((UNITS, 2, 2, 32, 768), bf),
            v((UNITS, 2, 2, 16, 768), f32), v((UNITS, 2, 16, 768), bf), v((UNITS, 2, 16, 768), bf),
            v((UNITS, 2, 16, 768), bf), v((16, 16, 768), bf),
            v((16, 16, 768), bf), v((16, 16, 768), bf), v((8, 2, 256, 128), bf), v((8, 2, 768, 128), bf),
            v((64, 768), f32), v((64, 2048), f32), v((16, 16, 128), f32), v((16, 16, 128), f32),
            v((16, 16, 128), f32), v((256, 64), f32),
            v((256, 768), f32), v((16, 16, 768), bf), v((16, 16, 768), bf),
            v((16, 32, 128), f32), v((16, 32, 128), bf), v((16, 32, 128), bf), v((16, 16, 32, 128), bf), v((384, 128), f32),
            dma((8,)), dma((1,)), dma((7, 2)), dma((2,)),
            dma((1,)), dma((UNITS,)), dma((1,)), dma((UNITS, 2)), dma((1,)), dma((UNITS, 2)),
            dma((1,)), dma((UNITS,)), dma((2,)),
            *[dma((2,))] * 8, dma((1,)), dma((7,)), dma((2,)), dma((4,)), dma((1,)), dma((7, 2)),
        ],
        compiler_params=pltpu.CompilerParams(
            collective_id=0, has_side_effects=True, vmem_limit_bytes=58 * 1024 * 1024
        ),
        cost_estimate=pl.CostEstimate(flops=5_900_000_000, bytes_accessed=12_000_000, transcendentals=512),
    )(
        residual_grad.reshape(8, 2, 16, 768), shortcut, hidden_in.reshape(16, 16, 768), key_value_gradient,
        key_value_weight, adapter_down_matrix.T, adapter_up,
    )
    return result, down.astype(f32).T, up.astype(f32)


def solution(mesh):
    part = P("dp", "tensor")
    return jax.shard_map(
        shards, mesh=mesh, in_specs=(part,) * 5 + (P(), P()),
        out_specs=(P(("dp", "tensor"), None), P(), P()), check_vma=False,
    )
```

```python
import jax
import jax.numpy as jnp
from jax import lax
from jax.experimental import pallas as pl
from jax.experimental.pallas import tpu as pltpu
from jax.sharding import PartitionSpec as P

MESH = pl.DeviceIdType.MESH
UNITS = 8
LAGS = (1, 2, 4, 6)
epsilon = 1e-05
adapter_scale = 0.25


def place(xh, z, y, xl, c):
    return {"dp": xh * 8 + z, "tensor": (y * 2 + xl) * 2 + c}


def contract(a, b):
    return lax.dot_general(a, b, (((1,), (1,)), ((), ())), preferred_element_type=jnp.float32)


def multiply(a, b):
    return jnp.dot(a, b, preferred_element_type=jnp.float32)


def contract_first(a, b):
    return lax.dot_general(a, b, (((0,), (0,)), ((), ())), preferred_element_type=jnp.float32)


def split(value):
    hi = value.astype(jnp.bfloat16)
    return hi, (value - hi.astype(jnp.float32)).astype(jnp.bfloat16)


def whole_kernel(
    grad_ref, short_ref, hidden_ref, kv_ref, kvw_ref, down_ref, up_ref,
    out_ref, down_out, up_out,
    blocks, weights, core_out, core_in, own, y_out, far_in, y_in, pair, x_out, x_in, fin_out, fin_in,
    hidden, hidden_in, kv_all, w_ring, down_rows, up_rows, sums_out, sums_in, sums_all, back_keep,
    norm_sum, norm_out, norm_in, g_out, g_wire, g_in, g_all, g_rows,
    load_sem, a_send, a_recv, s_sem,
    core_send, core_recv, far_send, far_recv, near_send, near_recv, x_send, x_recv, f_sem,
    h_sem, k_sem, kc_sem, su_sem, sa_sem, n_sem, gs_sem, gd_sem, gt_send, gt_recv, gc_sem, t_sem, w_send, w_recv,
):
    p, q = lax.axis_index("dp"), lax.axis_index("tensor")
    xh, z = p // 8, p % 8
    y, xl, c = q // 4, (q // 2) % 2, q % 2

    def at(xh=xh, z=z, y=y, xl=xl, c=c):
        return place(xh, z, y, xl, c)

    up, down = at(z=(z + 1) % 8), at(z=(z + 7) % 8)
    core_peer = at(c=1 - c)
    xl_peer = at(xl=1 - xl)

    def local(source, target, i):
        return pltpu.make_async_copy(source, target, load_sem.at[i])

    loads = [local(grad_ref.at[:, h], blocks.at[7, h], h) for h in range(2)]
    loads.append(local(short_ref, weights.at[0], 2))
    loads.append(local(hidden_ref, hidden, 3))
    loads.append(local(hidden_ref.at[q], hidden_in.at[q], 4))
    loads.append(local(kv_ref, kv_all.at[q // 2, c], 5))
    loads.append(local(down_ref.at[:, pl.ds(pl.multiple_of(q * 768, 128), 768)], down_rows, 6))
    loads.append(local(up_ref, up_rows, 7))
    for l in loads:
        l.start()

    barrier = pltpu.get_barrier_semaphore()

    def each(body, count=16):
        def step(d, carry):
            body(d)
            return carry
        lax.fori_loop(1, count, step, 0)

    def turn(a, d):
        return lax.rem(a + d, 16)

    def greet(d):
        pl.semaphore_signal(barrier, inc=1, device_id={"dp": p, "tensor": turn(q, d)}, device_id_type=MESH)
        pl.semaphore_signal(barrier, inc=1, device_id={"dp": turn(p, d), "tensor": q}, device_id_type=MESH)

    each(greet)

    @pl.when(p != q)
    def _():
        pl.semaphore_signal(barrier, inc=1, device_id={"dp": q, "tensor": p}, device_id_type=MESH)

    for l in loads:
        l.wait()

    @pl.when(p != q)
    def _():
        pl.semaphore_wait(barrier, 31)

    @pl.when(p == q)
    def _():
        pl.semaphore_wait(barrier, 30)

    def remote(src, dst, send, recv, to):
        return pltpu.make_async_remote_copy(
            src_ref=src, dst_ref=dst, send_sem=send, recv_sem=recv, device_id=to, device_id_type=MESH
        )

    def group(ref, sems):
        return remote(ref, ref, sems.at[0], sems.at[1], core_peer)

    def ring_copy(buffer, send, recv, s, h):
        source = 7 if s < 2 else (4 + h if s == 6 else s - 2)
        way = (up, down)[h if s == 6 else s % 2]
        return remote(buffer.at[source, h], buffer.at[s, h], send.at[0], recv.at[s, h], way)

    def block_copy(s, h):
        return ring_copy(blocks, a_send, a_recv, s, h)

    def w_copy(s, h):
        return ring_copy(w_ring, w_send, w_recv, s, h)

    def ring_half(copy, t, h):
        if t == 3:
            copy(6, h).wait_recv()
            return
        for s in (2 * t, 2 * t + 1):
            copy(s, h).wait_recv()
            if s < 4:
                copy(s + 2, h).start()
            elif s - 4 == h:
                copy(6, h).start()

    def ring_step(copy, t):
        ring_half(copy, t, 0)
        ring_half(copy, t, 1)

    for h in range(2):
        for s in range(2):
            block_copy(s, h).start()

    def swap_copy():
        return remote(weights.at[0], weights.at[1], s_sem.at[0], s_sem.at[1], at(xh=1 - xh))

    swap_copy().start()

    def to_tensor(source, target, sems, d):
        return remote(source, target, sems.at[0], sems.at[1], {"dp": p, "tensor": turn(q, d)})

    def to_dp(source, target, sems, d):
        return remote(source, target, sems.at[0], sems.at[1], {"dp": turn(p, d), "tensor": q})

    def turn_copy(part):
        return remote(kvw_ref, w_ring.at[7, part], t_sem.at[0], t_sem.at[1], {"dp": q, "tensor": p})

    def turn_local():
        return pltpu.make_async_copy(kvw_ref, w_ring.at[7, xh], t_sem.at[0])

    def half_copy(part):
        return remote(w_ring.at[7, part], w_ring.at[7, part], t_sem.at[2], t_sem.at[3], at(xh=1 - xh))

    @pl.when(p != q)
    def _():
        turn_copy(q // 8).start()

    @pl.when(p == q)
    def _():
        turn_local().start()

    down_hi, down_lo = split(down_rows[...])
    mine = hidden[...].reshape(256, 768)
    low = contract(mine, jnp.concatenate([down_hi, down_lo], axis=0))
    wide = mine.astype(jnp.float32)
    squares = jnp.sum(wide * wide, axis=1, keepdims=True)
    sums = jnp.concatenate([low[:, :64] + low[:, 64:], jnp.broadcast_to(squares, (256, 64))], axis=1)
    sums_out[...] = sums.reshape(16, 16, 128)
    each(lambda d: to_tensor(sums_out.at[turn(q, d)], sums_in.at[q], su_sem, d).start())
    sums_in[q] = sums_out[q]

    def kv_send():
        each(lambda e: to_tensor(kv_ref, kv_all.at[q // 2, c], k_sem, 2 * e).start(), 8)

    def kv_core_copy():
        return remote(kv_all.at[:, c], kv_all.at[:, c], kc_sem.at[0], kc_sem.at[1], core_peer)

    def kv_forward():
        group(kv_all.at[pl.ds(0, 7), 0], k_sem).wait_recv()
        kv_core_copy().start()

    def hidden_send():
        each(lambda d: to_tensor(hidden_ref.at[turn(q, d)], hidden_in.at[q], h_sem, d).start())

    def sums_reduce():
        group(sums_in.at[pl.ds(0, 15)], su_sem).wait_recv()
        sums_all[q] = jnp.sum(sums_in[...], axis=0)
        each(lambda d: to_tensor(sums_all.at[q], sums_all.at[q], sa_sem, d).start())

    def adapter_parts():
        group(sums_all.at[pl.ds(0, 15)], sa_sem).wait_recv()
        kv_core_copy().wait_recv()
        both = jnp.zeros((256, 128), jnp.float32)
        for s in range(16):
            hi, lo = split(up_rows[:, 128 * s : 128 * s + 128])
            both = both + contract(kv_all[s // 2, s % 2], jnp.concatenate([hi, lo], axis=0))
        back = both[:, :64] + both[:, 64:]
        back_keep[...] = back
        reduced = sums_all[...].reshape(256, 128)
        scale = lax.rsqrt(reduced[:, 64:65] / 12288 + epsilon)
        low = jnp.concatenate(split(scale * reduced[:, :64]), axis=1)
        upper = contract_first(low, kv_all[q // 2, c])
        g_out[8:16, 24:32] = jnp.zeros((8, 8, 128), jnp.float32)
        g_out[0:8, 24:32] = (adapter_scale * (upper[:64] + upper[64:])).reshape(8, 8, 128)
        scaled = jnp.concatenate(split(scale * back), axis=1)
        lower = contract_first(scaled, hidden[...].reshape(256, 768))
        lower = adapter_scale * (lower[:64] + lower[64:])
        for b in range(6):
            g_rows[64 * b : 64 * b + 64] = lower[:, 128 * b : 128 * b + 128]
        g_out[:, 0:24] = g_rows[...].reshape(16, 24, 128)
        g_wire[...] = g_out[...].astype(jnp.bfloat16)
        each(lambda d: to_dp(g_wire.at[turn(p, d)], g_in.at[p], gs_sem, d).start())
        g_in[p] = g_wire[p]

    def grads_reduce():
        group(g_in.at[pl.ds(0, 15)], gs_sem).wait_recv()
        g_all[q, p] = jnp.sum(g_in[...].astype(jnp.float32), axis=0).astype(jnp.bfloat16)
        each(lambda d: to_dp(g_all.at[q, p], g_all.at[q, p], gd_sem, d).start())

    def chips_copy(s, e):
        return remote(
            g_all.at[s], g_all.at[s], gt_send.at[0], gt_recv.at[e - 1], {"dp": p, "tensor": turn(q, 2 * e)}
        )

    def other_core_copy(s):
        return remote(g_all.at[s], g_all.at[s], gc_sem.at[0], gc_sem.at[1], core_peer)

    def grads_spread():
        group(g_all.at[q, pl.ds(0, 15)], gd_sem).wait_recv()
        each(lambda e: chips_copy(q, e).start(), 8)
        other_core_copy(q).start()

    def grads_forward():
        def body(e):
            s = turn(q, 16 - 2 * e)
            chips_copy(s, e).wait_recv()
            other_core_copy(s).start()
        each(body, 8)

    def block_z(s):
        half = (s + 2) // 2
        return lax.rem(z + 8 + jnp.where(s == 7, 0, jnp.where(s % 2 == 0, -half, half)), 8)

    def norm_term(slots):
        left = [kv_all[4 * part + block_z(s) // 2, block_z(s) % 2] for s in slots for part in range(2)]
        right = [w_ring[s, part] for s in slots for part in range(2)]
        return contract(jnp.concatenate(left, axis=1), jnp.concatenate(right, axis=1))

    def norm_begin():
        half_copy(1 - xh).wait_recv()
        for h in range(2):
            for s in range(2):
                w_copy(s, h).start()

    def norm_half(t):
        ring_half(w_copy, t, 0)

    def norm_hop(t):
        ring_half(w_copy, t, 1)
        term = norm_term((2 * t, 2 * t + 1))
        norm_sum[...] = term if t == 0 else norm_sum[...] + term

    def norm_send():
        back_hi, back_lo = split(back_keep[...])
        down_hi, down_lo = split(down_rows[...])
        extra = multiply(
            jnp.concatenate([back_hi, back_lo], axis=1), jnp.concatenate([down_hi, down_hi], axis=0)
        ) + multiply(back_hi, down_lo)
        total = norm_sum[...] + adapter_scale * extra
        norm_out[...] = total.astype(jnp.bfloat16).reshape(16, 16, 768)
        each(lambda d: to_tensor(norm_out.at[turn(q, d)], norm_in.at[q], n_sem, d).start())
        norm_in[q] = norm_out[q]

    def turn_done():
        @pl.when(p != q)
        def _():
            turn_copy(xh).wait_recv()

        @pl.when(p == q)
        def _():
            turn_local().wait()

        half_copy(xh).start()

    def core_copy(i):
        return remote(core_out.at[i], core_in.at[i], core_send.at[0], core_recv.at[i], core_peer)

    def far_copy(i, way):
        return remote(
            y_out.at[i, (y + 2) % 4, way], far_in.at[i, way], far_send.at[0], far_recv.at[i, way],
            at(y=(y + 1 + 2 * way) % 4),
        )

    def near_copy(i, way):
        to = (y + 1 + 2 * way) % 4
        return remote(y_out.at[i, to], y_in.at[i, way], near_send.at[0], near_recv.at[i, way], at(y=to))

    def x_copy(i):
        return remote(x_out.at[i], x_in.at[i], x_send.at[0], x_recv.at[i], xl_peer)

    def side_of(i):
        return jnp.where(i > 4, 1, jnp.where(i == 3, 1, 0))

    def pair_of(i):
        return jnp.where(i > 4, i - 4, jnp.where(i == 4, 3, jnp.where(i == 3, 0, i)))

    def fin_slot(i):
        g = side_of(i)
        return (xh + g - 2 * xh * g) * 8 + z

    before = {
        0: [lambda: ring_step(block_copy, 0)],
        1: [lambda: ring_step(block_copy, 1)],
        2: [lambda: ring_step(block_copy, 2)],
        3: [lambda: swap_copy().wait_recv()],
        4: [lambda: ring_step(block_copy, 3)],
    }
    after = {
        0: [turn_done, kv_send, hidden_send],
        1: [sums_reduce],
        2: [norm_begin, kv_forward],
        4: [adapter_parts, lambda: norm_half(0)],
        5: [lambda: norm_hop(0)],
        6: [grads_reduce, lambda: norm_half(1)],
        7: [lambda: norm_hop(1)],
        8: [grads_spread, lambda: norm_half(2)],
        9: [lambda: norm_hop(2)],
        10: [lambda: norm_half(3), grads_forward],
        11: [lambda: norm_hop(3), norm_send],
    }

    def run(table, i):
        for when, acts in table.items():
            @pl.when(i == when)
            def _(acts=acts):
                for act in acts:
                    act()

    def step(i, carry):
        run(before, i)

        @pl.when(i < UNITS)
        def _():
            t, g = pair_of(i), side_of(i)
            both = contract(blocks[pl.ds(2 * t, 2)].reshape(512, 768), weights[g]).reshape(2, 2, 4, 32, 768)
            first, second = both[:, 0], both[:, 1]
            theirs = jnp.where(c == 0, second, first).astype(jnp.bfloat16)
            mine = jnp.where(c == 0, first, second)
            for b in range(2):
                core_out[i, :, b] = theirs[b]
            core_copy(i).start()
            for b in range(2):
                own[i, :, b] = mine[b]

        j = i - LAGS[0]

        @pl.when(jnp.logical_and(j >= 0, j < UNITS))
        def _():
            core_copy(j).wait_recv()
            total = own[j] + core_in[j].astype(jnp.float32)
            own[j] = total
            y_out[j] = total.astype(jnp.bfloat16)
            far_copy(j, 0).start()
            far_copy(j, 1).start()

        r = i - LAGS[1]

        @pl.when(jnp.logical_and(r >= 0, r < UNITS))
        def _():
            for way in range(2):
                far_copy(r, way).wait_recv()
                to = (y + 1 + 2 * way) % 4
                y_out[r, to, way] = (own[r, to, way] + far_in[r, way].astype(jnp.float32)).astype(jnp.bfloat16)
                near_copy(r, way).start()

        m = i - LAGS[2]

        @pl.when(jnp.logical_and(m >= 0, m < UNITS))
        def _():
            for way in range(2):
                near_copy(m, way).wait_recv()
            got = y_in[m].astype(jnp.float32)
            total = (own[m, y] + (got[0] + got[1])).reshape(2, 2, 16, 768)
            pair[m] = total
            for b in range(2):
                x_out[m, b] = pair[m, b, 1 - xl].astype(jnp.bfloat16)
            x_copy(m).start()

        n = i - LAGS[3]

        @pl.when(jnp.logical_and(n >= 0, n < UNITS))
        def _():
            x_copy(n).wait_recv()
            for b in range(2):
                done = (pair[n, b, xl] + x_in[n, b].astype(jnp.float32)).astype(jnp.bfloat16)
                s = 2 * pair_of(n) + b
                slot = fin_slot(n)

                @pl.when(s == 7)
                def _():
                    fin_in[slot] = done

                @pl.when(s != 7)
                def _():
                    fin_out[n, b] = done
                    remote(
                        fin_out.at[n, b], fin_in.at[slot], f_sem.at[0], f_sem.at[1], at(z=block_z(s))
                    ).start()

        run(after, i)
        return carry

    lax.fori_loop(0, UNITS + LAGS[3], step, 0)

    group(g_all.at[pl.ds(0, 8)], gc_sem).wait_recv()

    def unpack(s, carry):
        packed = g_all[s].astype(jnp.float32)
        lower = packed[:, :24].reshape(6, 64, 128)
        for b in range(6):
            down_out[:, pl.ds(pl.multiple_of(s * 768 + 128 * b, 128), 128)] = lower[b].astype(down_out.dtype)
        up_out[:, pl.ds(pl.multiple_of(s * 128, 128), 128)] = packed[:8, 24:].reshape(64, 128).astype(up_out.dtype)
        return carry

    lax.fori_loop(0, 16, unpack, 0)

    group(hidden_in.at[pl.ds(0, 15)], h_sem).wait_recv()
    group(norm_in.at[pl.ds(0, 15)], n_sem).wait_recv()
    my_scale = lax.rsqrt(sums_all[q][:, 64:65] / 12288 + epsilon)

    def dots(s, total):
        return total + hidden_in[s].astype(jnp.float32) * norm_in[s].astype(jnp.float32)

    products = lax.fori_loop(0, 16, dots, jnp.zeros((16, 768), jnp.float32))
    inner = jnp.sum(products, axis=1, keepdims=True) * my_scale / 12288
    group(fin_in.at[pl.ds(0, 14)], f_sem).wait_recv()

    def take(s, carry):
        normed = hidden_in[s].astype(jnp.float32) * my_scale
        done = fin_in[s].astype(jnp.float32) + my_scale * (norm_in[s].astype(jnp.float32) - normed * inner)
        out_ref[:, pl.ds(pl.multiple_of(s * 768, 128), 768)] = done.astype(out_ref.dtype)
        return carry

    lax.fori_loop(0, 16, take, 0)

    def gone(ref, sems):
        remote(ref, ref, sems.at[0], sems.at[0], core_peer).wait_send()

    gone(blocks.at[pl.ds(0, 7)], a_send)
    gone(w_ring.at[pl.ds(0, 7)], w_send)
    swap_copy().wait_send()
    gone(core_out, core_send)
    gone(far_in, far_send)
    gone(y_in, near_send)
    gone(x_out, x_send)
    gone(fin_in.at[pl.ds(0, 14)], f_sem)
    half_copy(xh).wait_send()

    @pl.when(p != q)
    def _():
        turn_copy(q // 8).wait_send()

    gone(sums_in.at[pl.ds(0, 15)], su_sem)
    gone(sums_all.at[pl.ds(0, 15)], sa_sem)
    gone(kv_all.at[pl.ds(0, 7), 0], k_sem)
    kv_core_copy().wait_send()
    gone(hidden_in.at[pl.ds(0, 15)], h_sem)
    gone(norm_in.at[pl.ds(0, 15)], n_sem)
    gone(g_in.at[pl.ds(0, 15)], gs_sem)
    gone(g_all.at[0, pl.ds(0, 15)], gd_sem)
    gone(g_all.at[pl.ds(0, 7)], gt_send)
    gone(g_all.at[pl.ds(0, 8)], gc_sem)


def shards(hidden_in, residual_grad, key_value_gradient, shortcut, key_value_weight, adapter_down_matrix, adapter_up):
    bf, f32, dma = jnp.bfloat16, jnp.float32, pltpu.SemaphoreType.DMA
    v = pltpu.VMEM
    result, down, up = pl.pallas_call(
        whole_kernel,
        out_shape=[
            jax.ShapeDtypeStruct((16, 12288), bf),
            jax.ShapeDtypeStruct((64, 12288), bf),
            jax.ShapeDtypeStruct((64, 2048), bf),
        ],
        in_specs=[pl.BlockSpec(memory_space=pl.ANY)] * 7,
        out_specs=[pl.BlockSpec(memory_space=pltpu.VMEM)] * 3,
        scratch_shapes=[
            v((8, 2, 8, 16, 768), bf), v((2, 768, 768), bf),
            v((UNITS, 4, 2, 32, 768), bf), v((UNITS, 4, 2, 32, 768), bf), v((UNITS, 4, 2, 32, 768), f32),
            v((UNITS, 4, 2, 32, 768), bf), v((UNITS, 2, 32, 768), bf), v((UNITS, 2, 2, 32, 768), bf),
            v((UNITS, 2, 2, 16, 768), f32), v((UNITS, 2, 16, 768), bf), v((UNITS, 2, 16, 768), bf),
            v((UNITS, 2, 16, 768), bf), v((16, 16, 768), bf),
            v((16, 16, 768), bf), v((16, 16, 768), bf), v((8, 2, 256, 128), bf), v((8, 2, 768, 128), bf),
            v((64, 768), f32), v((64, 2048), f32), v((16, 16, 128), f32), v((16, 16, 128), f32),
            v((16, 16, 128), f32), v((256, 64), f32),
            v((256, 768), f32), v((16, 16, 768), bf), v((16, 16, 768), bf),
            v((16, 32, 128), f32), v((16, 32, 128), bf), v((16, 32, 128), bf), v((16, 16, 32, 128), bf), v((384, 128), f32),
            dma((8,)), dma((1,)), dma((7, 2)), dma((2,)),
            dma((1,)), dma((UNITS,)), dma((1,)), dma((UNITS, 2)), dma((1,)), dma((UNITS, 2)),
            dma((1,)), dma((UNITS,)), dma((2,)),
            *[dma((2,))] * 8, dma((1,)), dma((7,)), dma((2,)), dma((4,)), dma((1,)), dma((7, 2)),
        ],
        compiler_params=pltpu.CompilerParams(
            collective_id=0, has_side_effects=True, vmem_limit_bytes=58 * 1024 * 1024
        ),
        cost_estimate=pl.CostEstimate(flops=5_900_000_000, bytes_accessed=12_000_000, transcendentals=512),
    )(
        residual_grad.reshape(8, 2, 16, 768), shortcut, hidden_in.reshape(16, 16, 768), key_value_gradient,
        key_value_weight, adapter_down_matrix.T, adapter_up,
    )
    return result, down.astype(f32).T, up.astype(f32)


def solution(mesh):
    part = P("dp", "tensor")
    return jax.shard_map(
        shards, mesh=mesh, in_specs=(part,) * 5 + (P(), P()),
        out_specs=(P(("dp", "tensor"), None), P(), P()), check_vma=False,
    )
```
